512 devices in a mesh: dp: 4 (over y_hi, core), seq: 128 (over x, z, y_lo).
Axes of the slice: x: 4, y: 8 (y_hi: 2, y_lo: 4; y = y_hi * 4 + y_lo), z: 8, core: 2. Of those that a mesh axis runs over, the one named last changes fastest.
Arguments:
- queries: bfloat16 [65536, 768], P(('dp', 'seq')), parts along dimension 0, may hold values from -6 to 6
- keys: bfloat16 [65536, 768], P(('dp', 'seq')), parts along dimension 0, may hold values from -6 to 6
- values: bfloat16 [65536, 768], P(('dp', 'seq')), parts along dimension 0, may hold values from -16 to 16
- cotangent: bfloat16 [65536, 768], P(('dp', 'seq')), parts along dimension 0, may hold values from -24 to 24
- out_weight: bfloat16 [768, 768], replicated, may hold values from -0.21875 to 0.21875
- slide_lengths: int32 [32], P('dp'), parts along dimension 0, may hold values from 1 to 4096, 16384 in all
- head_dilation_shifts: int32 [2, 16], replicated, may hold values from 0 to 15, as said below
Outputs:
- mixed: bfloat16 [65536, 768], P(('dp', 'seq')), parts along dimension 0
- grad_queries: bfloat16 [65536, 768], P(('dp', 'seq')), parts along dimension 0
- grad_keys: bfloat16 [65536, 768], P(('dp', 'seq')), parts along dimension 0
- grad_values: bfloat16 [65536, 768], P(('dp', 'seq')), parts along dimension 0
- out_weight_grad: float32 [3072, 768], P(('dp', 'seq')), parts along dimension 0
The draws below stay inside these ranges and needn't reach their ends.
There are 4 independent parts, one for each index of `dp`. The reference program is written for one: setup_inputs(seed, part) draws one part's arguments, and reference() takes and returns one part's arrays. A program takes and returns all parts, laid end to end along the dimension named above; an argument that names none is the same for every part. Nothing has to cross between parts.
Inputs may be any that keep to these rules, and one draw needn't show every extreme that they name: `head_dilation_shifts`: row 0 holds each head's offset at level two, below 4; row 1 each head's offset at level three, below 16.
All inputs are finite; a program needn't handle non-finite values.
Results may differ from the reference program's by a relative error of at most 0.012.
The reference program's roundings to bfloat16 on the way count: a program that leaves them out, or rounds other values in their place, can miss the bound.
Values may be sent and summed in bfloat16 or wider, within the bound.
A program may use at most 64 MiB of HBM per device.

```python
import math
from functools import partial
import jax
import jax.numpy as jnp
import numpy as np
from jax import lax

D = 768
ATTENTION_HEADS = 16
SLIDES = 8
DILATION_TWO = 4
DILATION_THREE = 16
TOKENS = 16384
SEGMENT_ONE = 128
SEGMENT_TWO = 1024
SEGMENT_THREE = 4096
MOST = 4096


def draw_keys(key, part):
    own_key = jax.random.fold_in(key, 3)
    return jnp.clip(jax.random.normal(own_key, (TOKENS, D), jnp.float32), -6.0, 6.0).astype(jnp.bfloat16)


def draw_queries(key, part):
    own_key = jax.random.fold_in(key, 5)
    return jnp.clip(jax.random.normal(own_key, (TOKENS, D), jnp.float32), -6.0, 6.0).astype(jnp.bfloat16)


def draw_head_dilation_shifts(key, part):
    key = jax.random.fold_in(key, 7)
    permuted_rows = jax.random.permutation(key, ATTENTION_HEADS).astype(jnp.int32)
    return jnp.stack([permuted_rows % DILATION_TWO, permuted_rows % DILATION_THREE]).astype(jnp.int32)


def raised(values, stream_key, source, target, blocks, factor):
    owner, partner = [(jnp.arange(values.shape[position]) // (values.shape[position] // blocks)).reshape([-1 if axis == position else 1 for axis in range(values.ndim)]) for position in (source, target)]
    chosen = jax.random.permutation(stream_key, blocks)[partner]
    strong = (owner == chosen) | (owner == (partner + blocks // 2) % blocks)
    return jnp.where(strong, factor * values, values)


def block_scale(stream_key, shape, cuts, least, top_value):
    gain = 1.0
    for axis_at, shards_of in cuts:
        draws = jax.random.uniform(jax.random.fold_in(jax.random.fold_in(stream_key, 6), axis_at), (shards_of,), jnp.float32, least / len(cuts), top_value / len(cuts))
        gain = gain * jnp.repeat(jnp.exp(draws), shape[axis_at] // shards_of).reshape((-1,) + (1,) * (len(shape) - 1 - axis_at))
    return gain


def profile(number_of, total, limit, skew):
    loads = [(1 << 20) // math.isqrt(standing ** skew) + 1 for standing in range(2, number_of + 1)]
    rest, holding = total - limit - (number_of - 1), [1] * (number_of - 1)
    while rest > 0:
        candidates = [i for i in range(number_of - 1) if holding[i] < limit]
        pool, budget = sum([loads[i] for i in candidates]), rest
        for i in candidates:
            more = min(limit - holding[i], max(1, budget * loads[i] // pool), rest)
            holding[i] = holding[i] + more
            rest = rest - more
    return np.array([limit] + holding)


def uneven(key, amount, total, most, skew):
    if amount == 2:
        one = jax.random.randint(key, (), max(1, total - most), min(most, total - 1) + 1)
        return jnp.stack([one, total - one])
    lengths = jnp.asarray(profile(amount, total, most, skew), jnp.int32)
    couples = (amount - 1) // 2
    source_of, taker = lengths[1:1 + 2 * couples:2], lengths[2:2 + 2 * couples:2]
    room = jnp.minimum(source_of - 1, most - taker)
    shifted = jax.random.randint(jax.random.fold_in(key, 1), (couples,), 0, 1 << 20) % (room + 1)
    lengths = lengths.at[1:1 + 2 * couples:2].set(source_of - shifted).at[2:2 + 2 * couples:2].set(taker + shifted)
    return lengths[jax.random.permutation(jax.random.fold_in(key, 2), amount)]


def gaussian(key, dims, deviation, limit, shards=(), held_as=jnp.bfloat16):
    values = jax.random.normal(key, dims, jnp.float32) * deviation
    if len(shards) > 0:
        values = block_scale(key, dims, shards, -0.22, 0.18) * values
    return jnp.clip(values, min=-limit, max=limit).astype(held_as)


def heavy_noise(rng, shape, scale, limit, cuts, heavy, held_as=jnp.bfloat16):
    values = scale * jax.random.normal(rng, shape, jnp.float32)
    if cuts:
        values = values * block_scale(rng, shape, cuts, -0.22, 0.18)
    return jnp.clip(raised(values, jax.random.fold_in(rng, 3), *heavy), -limit, limit).astype(held_as)


def setup_inputs(seed: int = 0, part: int = 0) -> dict:
    splits = jax.random.split(jax.random.key(seed), 8)
    part_splits = jax.random.split(jax.random.fold_in(splits[7], part), 8)
    queries = draw_queries(jax.random.fold_in(jax.random.fold_in(splits[7], part), 71), part)
    keys = draw_keys(jax.random.fold_in(jax.random.fold_in(splits[7], part), 71), part)
    values = gaussian(part_splits[2], (TOKENS, D), 4.0, 16.0, ((0, 128),))
    cotangent = heavy_noise(part_splits[3], (TOKENS, D), 1.0, 24.0, ((0, 128),), (0, 1, 128, 5.5))
    out_weight = gaussian(splits[4], (D, D), D ** -0.5, 0.21875)
    slide_lengths = uneven(part_splits[5], SLIDES, TOKENS, MOST, 2).astype(jnp.int32)
    head_dilation_shifts = draw_head_dilation_shifts(jax.random.fold_in(splits[7], 71), part)
    return dict(queries=queries, keys=keys, values=values, cotangent=cotangent, out_weight=out_weight, slide_lengths=slide_lengths, head_dilation_shifts=head_dilation_shifts)


def slide_index(positions, slide_ends):
    return jnp.sum((positions[..., None] >= slide_ends).astype(jnp.int32), axis=-1)


def pick(array, rate, shifts):
    if rate == 1:
        return array
    rows = array.reshape((array.shape[0] // rate, rate) + array.shape[1:])
    chosen = jnp.arange(rate, dtype=jnp.int32)[:, None] == shifts[None, :]
    chosen = chosen.reshape(chosen.shape + (1,) * (array.ndim - 2))
    return jnp.sum(jnp.where(chosen[None], rows, jnp.zeros((), array.dtype)), axis=1).astype(array.dtype)


def spread(selected, rate, shifts, fill):
    if rate == 1:
        return selected
    chosen = jnp.arange(rate, dtype=jnp.int32)[:, None] == shifts[None, :]
    chosen = chosen.reshape(chosen.shape + (1,) * (selected.ndim - 2))
    wide = jnp.where(chosen[None], selected[:, None], fill)
    return wide.reshape((selected.shape[0] * rate,) + selected.shape[1:])


def level_forward(block, scale):
    query_rows, key_rows, value_rows, slides = block
    scores = jnp.einsum("qhd,khd->hqk", query_rows.astype(jnp.float32), key_rows.astype(jnp.float32)) * scale
    visible = slides.T[:, :, None] == slides.T[:, None, :]
    highest = jnp.max(jnp.where(visible, scores, -jnp.inf), axis=-1)
    weights = jnp.where(visible, jnp.exp(scores - highest[..., None]), 0.0)
    totals = jnp.sum(weights, axis=-1)
    rounded = weights.astype(jnp.bfloat16)
    summed = jnp.einsum("hqk,khd->qhd", rounded.astype(jnp.float32), value_rows.astype(jnp.float32))
    return highest.T, totals.T, summed


def level_backward(block, scale):
    query_rows, key_rows, value_rows, grad_rows, lse_rows, delta_rows, slides = block
    scores = jnp.einsum("qhd,khd->hqk", query_rows.astype(jnp.float32), key_rows.astype(jnp.float32)) * scale
    visible = slides.T[:, :, None] == slides.T[:, None, :]
    probs = jnp.where(visible, jnp.exp(scores - lse_rows.T[:, :, None]), 0.0)
    dprobs = jnp.einsum("qhd,khd->hqk", grad_rows.astype(jnp.float32), value_rows.astype(jnp.float32))
    dscores = (probs * (dprobs - delta_rows.T[:, :, None]) * scale).astype(jnp.bfloat16).astype(jnp.float32)
    grad_q = jnp.einsum("hqk,khd->qhd", dscores, key_rows.astype(jnp.float32))
    grad_k = jnp.einsum("hqk,qhd->khd", dscores, query_rows.astype(jnp.float32))
    grad_v = jnp.einsum("hqk,qhd->khd", probs.astype(jnp.bfloat16).astype(jnp.float32), grad_rows.astype(jnp.float32))
    return grad_q, grad_k, grad_v


def segments(array, length):
    return array.reshape((-1, length) + array.shape[1:])


def reference(queries, keys, values, cotangent, out_weight, slide_lengths, head_dilation_shifts):
    head_dim = D // ATTENTION_HEADS
    scale = head_dim ** -0.5
    slide_ends = jnp.cumsum(slide_lengths).astype(jnp.int32)
    level_layouts = [(1, SEGMENT_ONE, jnp.zeros((ATTENTION_HEADS,), jnp.int32)), (DILATION_TWO, SEGMENT_TWO, head_dilation_shifts[0].astype(jnp.int32)), (DILATION_THREE, SEGMENT_THREE, head_dilation_shifts[1].astype(jnp.int32))]
    views = [array.reshape(TOKENS, ATTENTION_HEADS, head_dim) for array in (queries, keys, values)]
    stored = []
    highs, sums, partials = [], [], []
    for rate, length, shifts in level_layouts:
        picked = [pick(array, rate, shifts) for array in views]
        positions = jnp.arange(TOKENS // rate, dtype=jnp.int32)[:, None] * rate + shifts[None, :]
        slides = slide_index(positions, slide_ends)
        stored.append((picked, slides))
        block = tuple(segments(array, length // rate) for array in picked + [slides])
        highest, totals, summed = lax.map(partial(level_forward, scale=scale), block)
        highs.append(spread(highest.reshape(-1, ATTENTION_HEADS), rate, shifts, -jnp.inf))
        sums.append(spread(totals.reshape(-1, ATTENTION_HEADS), rate, shifts, 0.0))
        partials.append(spread(summed.reshape(-1, ATTENTION_HEADS, head_dim), rate, shifts, 0.0))
    best = highs[0]
    for highest in highs[1:]:
        best = jnp.maximum(best, highest)
    mass = jnp.zeros((TOKENS, ATTENTION_HEADS), jnp.float32)
    for highest, totals in zip(highs, sums):
        mass = mass + jnp.exp(highest - best) * totals
    lse = best + jnp.log(mass)
    combined = jnp.zeros((TOKENS, ATTENTION_HEADS, head_dim), jnp.float32)
    for highest, summed in zip(highs, partials):
        combined = combined + jnp.exp(highest - lse)[..., None] * summed
    attended = combined.reshape(TOKENS, D).astype(jnp.bfloat16)
    mixed = jnp.dot(attended, out_weight.T, preferred_element_type=jnp.float32).astype(jnp.bfloat16)
    d_attended = jnp.dot(cotangent, out_weight, preferred_element_type=jnp.float32).astype(jnp.bfloat16)
    delta = jnp.sum((d_attended.astype(jnp.float32) * attended.astype(jnp.float32)).reshape(TOKENS, ATTENTION_HEADS, head_dim), axis=-1)
    d_view = d_attended.reshape(TOKENS, ATTENTION_HEADS, head_dim)
    grads = [jnp.zeros((TOKENS, ATTENTION_HEADS, head_dim), jnp.float32) for index in range(3)]
    for (rate, length, shifts), (picked, slides) in zip(level_layouts, stored):
        extra = [pick(d_view, rate, shifts), pick(lse, rate, shifts), pick(delta, rate, shifts)]
        block = tuple(segments(array, length // rate) for array in picked + extra + [slides])
        results = lax.map(partial(level_backward, scale=scale), block)
        grads = [total + spread(result.reshape(-1, ATTENTION_HEADS, head_dim), rate, shifts, 0.0) for total, result in zip(grads, results)]
    grad_queries, grad_keys, grad_values = [total.reshape(TOKENS, D).astype(jnp.bfloat16) for total in grads]
    out_weight_grad = jnp.dot(cotangent.T, attended, preferred_element_type=jnp.float32) * (TOKENS ** -0.5)
    return mixed, grad_queries, grad_keys, grad_values, out_weight_grad
```

```python
import jax
import jax.numpy as jnp
from jax import lax
from jax.experimental import pallas as pl
from jax.experimental.pallas import tpu as pltpu
from jax.sharding import PartitionSpec as P

HEADS = 16
DIM = 48
WIDTH = HEADS * DIM
ROWS = 128
TILES = WIDTH // 128
HALF = WIDTH // 2
RATE = (4, 16)
COUNT = (ROWS // 4, ROWS // 16)
SCALE = DIM**-0.5
HIDDEN = -1e30
F32 = jnp.float32
BF16 = jnp.bfloat16
MESH = pl.DeviceIdType.MESH


def matmul(a, b, contract):
    return lax.dot_general(a, b, ((contract[:1], contract[1:]), ((), ())), preferred_element_type=F32)


def iota(shape, axis):
    return lax.broadcasted_iota(jnp.int32, shape, axis)


def over_48(columns):
    return (columns * 1366) >> 16


def tile_span(first, width):
    return range(first // 128, (first + width - 1) // 128 + 1)


def take_window(tiles, first, width, place):
    at, off = first // 128, first % 128
    turn = (place - off) % 128
    near = tiles[at] if turn == 0 else pltpu.roll(tiles[at], turn, 1)
    if off + width <= 128:
        return near
    far = tiles[at + 1] if turn == 0 else pltpu.roll(tiles[at + 1], turn, 1)
    return jnp.where(iota(near.shape, 1) < place + 128 - off, near, far)


def put_windows(windows, width, place):
    tiles = [None] * TILES
    for index, window in enumerate(windows):
        first = index * width
        off = first % 128
        turn = (off - place) % 128
        turned = window if turn == 0 else pltpu.roll(window, turn, 1)
        for tile in tile_span(first, width):
            if tiles[tile] is None:
                tiles[tile] = turned
            else:
                columns = iota(window.shape, 1) + 128 * tile
                inside = (columns >= first) & (columns < first + width)
                tiles[tile] = jnp.where(inside, turned, tiles[tile])
    return tiles


def three_parts(value):
    high = value.astype(BF16).astype(F32)
    rest = value - high
    middle = rest.astype(BF16).astype(F32)
    return high, middle, rest - middle


def kernel(
    q_ref,
    k_ref,
    v_ref,
    cot_ref,
    weight_ref,
    length_ref,
    shift_ref,
    mixed_ref,
    dq_ref,
    dk_ref,
    dv_ref,
    dw_ref,
    source,
    send_two,
    recv_two,
    send_three,
    recv_three,
    out_send_two,
    out_recv_two,
    out_send_three,
    out_recv_three,
    stat_send_two,
    stat_recv_two,
    stat_send_three,
    stat_recv_three,
    grad_send_two,
    grad_recv_two,
    grad_send_three,
    grad_recv_three,
    cot_halves,
    att_halves,
    cot_all,
    att_all,
    part,
    z_send,
    z_recv,
    y_send,
    y_recv,
    scores_one,
    scores_two,
    scores_three,
    level_out,
    level_lse,
    lse_wide,
    delta_wide,
    totals,
    send_sems,
    recv_sems,
):
    rank = lax.axis_index("seq")
    x, z, y = rank // 32, (rank % 32) // 4, rank % 4
    x_high, x_low = x // 2, x % 2
    plane, mine_three = rank - rank % 32, rank % 32
    block, mine_two = rank - rank % 8, rank % 8
    has_head = mine_three % 2 == (mine_three // 4) % 2
    own_head = mine_three // 2

    def worker(head):
        return 2 * head + (head // 2) % 2

    barrier = pltpu.get_barrier_semaphore()

    def greet(device):
        pl.semaphore_signal(barrier, inc=1, device_id={"seq": device}, device_id_type=MESH)

    @pl.loop(1, 32)
    def _(step):
        greet(plane + (mine_three + step) % 32)

    @pl.loop(1, 4)
    def _(step):
        greet(((x + step) % 4) * 32 + mine_three)

    other_x = 2 * x_high + 1 - x_low

    @pl.loop(1, 4)
    def _(step):
        greet(other_x * 32 + z * 4 + (y + step) % 4)

    def push(from_ref, to_ref, index, device):
        pltpu.make_async_remote_copy(
            src_ref=from_ref,
            dst_ref=to_ref,
            send_sem=send_sems.at[index],
            recv_sem=recv_sems.at[index],
            device_id={"seq": device},
            device_id_type=MESH,
        ).start()

    def keep(from_ref, to_ref, index):
        pltpu.make_async_copy(from_ref, to_ref, recv_sems.at[index]).start()

    def arrived(ref, index):
        pltpu.make_async_copy(ref, ref, recv_sems.at[index]).wait()

    def left(ref, index):
        pltpu.make_async_copy(ref, ref, send_sems.at[index]).wait()

    d_attended = jnp.dot(cot_ref[...], weight_ref[...], preferred_element_type=F32).astype(BF16)
    for index, ref in enumerate((q_ref, k_ref, v_ref, None)):
        for tile in range(TILES):
            lanes = slice(128 * tile, 128 * tile + 128)
            value = d_attended[:, lanes] if ref is None else ref[:, lanes]
            source[index, tile] = value.astype(F32)
    cot_halves[0] = cot_ref[:, :HALF]
    cot_halves[1] = cot_ref[:, HALF:]

    def column_shift(level, tile):
        shape = (COUNT[level], 128)
        heads = over_48(iota(shape, 1) + 128 * tile)
        value = jnp.zeros(shape, jnp.int32)
        for head in range(HEADS):
            if tile in tile_span(head * DIM, DIM):
                value = jnp.where(heads == head, shift_ref[level, head], value)
        return value

    shifts = [[column_shift(level, tile) for tile in range(TILES)] for level in range(2)]

    def pick(view, level):
        tiles = []
        for tile in range(TILES):
            value = view[tile, pl.ds(0, COUNT[level], RATE[level]), :]
            for offset in range(1, RATE[level]):
                rows = view[tile, pl.ds(offset, COUNT[level], RATE[level]), :]
                value = jnp.where(shifts[level][tile] == offset, rows, value)
            tiles.append(value)
        return tiles

    def spread(view, level, tiles, add):
        for tile in range(TILES):
            for offset in range(RATE[level]):
                place = (tile, pl.ds(offset, COUNT[level], RATE[level]), slice(None))
                other = view[place] if add else HIDDEN
                value = tiles[tile] + other if add else tiles[tile]
                view[place] = jnp.where(shifts[level][tile] == offset, value, other)

    picked_three = [pick(source.at[index], 1) for index in range(4)]
    for head in range(HEADS):
        low = iota((8, 128), 1) < 64
        for half in range(2):
            near = take_window(picked_three[2 * half], head * DIM, DIM, 0)
            far = take_window(picked_three[2 * half + 1], head * DIM, DIM, 64)
            totals[0, 0, 8 * half : 8 * half + 8] = jnp.where(low, near, far)
        send_three[head] = totals[0, 0, 0:16].astype(BF16)
    for index in range(4):
        picked = pick(source.at[index], 0)
        for other in range(8):
            send_two[other, index] = take_window(picked, 96 * other, 96, 0).astype(BF16)

    pl.semaphore_wait(barrier, 37)

    @pl.loop(1, 8)
    def _(step):
        other = (mine_two + step) % 8
        push(send_two.at[other], recv_two.at[:, pl.ds(32 * mine_two, 32)], 0, block + other)

    keep(send_two.at[mine_two], recv_two.at[:, pl.ds(32 * mine_two, 32)], 0)

    @pl.loop(0, HEADS)
    def _(step):
        head = (own_head + step) % HEADS
        other = worker(head)

        @pl.when(other != mine_three)
        def _():
            push(send_three.at[head], recv_three.at[mine_three], 1, plane + other)

    @pl.when(has_head)
    def _():
        keep(send_three.at[own_head], recv_three.at[mine_three], 1)

    @pl.loop(1, 4)
    def _(step):
        other = (x + step) % 4
        push(cot_halves.at[other // 2], cot_all.at[x], 2, other * 32 + mine_three)

    keep(cot_halves.at[x_high], cot_all.at[x], 2)

    ends = []
    running = 0
    for index in range(8):
        running = running + length_ref[index]
        ends.append(running)

    def slide(positions):
        value = jnp.zeros(positions.shape, jnp.int32)
        for end in ends:
            value = value + jnp.where(positions >= end, 1, 0)
        return value

    def seen(count, first, stride):
        rows = slide(first + stride * iota((count, 128), 0))
        columns = slide(first + stride * iota((8, count), 1))[0:1]
        rows = jnp.concatenate([rows] * (count // 128), axis=1)
        return rows == jnp.broadcast_to(columns, (count, count))

    def lane_mask(shape, first, width):
        lanes = iota(shape, 1)
        return (lanes >= first) & (lanes < first + width)

    def masked(value, first, width):
        inside = lane_mask(value.shape, first, width)
        return jnp.where(inside, value.astype(F32), 0.0).astype(BF16)

    def window(head):
        span = tile_span(head * DIM, DIM)
        return slice(128 * span[0], 128 * (span[-1] + 1)), head * DIM - 128 * span[0], span

    visible_one = seen(ROWS, ROWS * rank, 1)
    outs, tops, sums = ([None] * TILES for _ in range(3))

    def merge(tiles, head, value, wide):
        _, first, span = window(head)
        for index, tile in enumerate(span):
            piece = value[:, 128 * index : 128 * index + 128] if wide else value
            piece = jnp.broadcast_to(piece, (ROWS, 128))
            if tiles[tile] is None:
                tiles[tile] = piece
            else:
                columns = iota((ROWS, 128), 1) + 128 * index
                inside = (columns >= first) & (columns < first + DIM)
                tiles[tile] = jnp.where(inside, piece, tiles[tile])

    for head in range(HEADS):
        lanes, first, span = window(head)
        scores = matmul(masked(q_ref[:, lanes], first, DIM), k_ref[:, lanes], (1, 1)) * SCALE
        scores = jnp.where(visible_one, scores, HIDDEN)
        scores_one[head] = scores
        top = jnp.max(scores, axis=1, keepdims=True)
        weights = jnp.exp(scores - top)
        total = jnp.sum(weights, axis=1, keepdims=True)
        out = matmul(weights.astype(BF16), v_ref[:, lanes], (1, 0))
        merge(outs, head, out, True)
        merge(tops, head, top, False)
        merge(sums, head, total, False)
    for tile in range(TILES):
        level_out[0, tile] = outs[tile] / sums[tile]
        level_lse[0, tile] = tops[tile] + jnp.log(sums[tile])

    def split_three():
        both = recv_three[...].astype(F32).reshape(32, 2, 8, 128)
        first = both[:, 0].reshape(256, 128)
        second = both[:, 1].reshape(256, 128)
        return first, second, pltpu.roll(first, 64, 1), pltpu.roll(second, 64, 1)

    def part_of(value, first):
        return jnp.where(lane_mask(value.shape, first, DIM), value, 0.0).astype(BF16)

    @pl.when(has_head)
    def _():
        arrived(recv_three, 1)
        first, second, first_turned, second_turned = split_three()
        scores = matmul(part_of(first, 0), first_turned.astype(BF16), (1, 1)) * SCALE
        visible = seen(256, 4096 * x + shift_ref[1, own_head], RATE[1])
        scores = jnp.where(visible, scores, HIDDEN)
        scores_three[...] = scores
        top = jnp.max(scores, axis=1, keepdims=True)
        weights = jnp.exp(scores - top)
        total = jnp.sum(weights, axis=1, keepdims=True)
        out = matmul(weights.astype(BF16), second.astype(BF16), (1, 0)) / total
        lse = jnp.broadcast_to(top + jnp.log(total), (256, 128))
        out = jnp.where(iota((256, 128), 1) < 64, out, lse)
        out_send_three[...] = out.reshape(32, 8, 128)

        @pl.loop(1, 32)
        def _(step):
            other = (mine_three + step) % 32
            push(out_send_three.at[other], out_recv_three.at[own_head], 3, plane + other)

        keep(out_send_three.at[mine_three], out_recv_three.at[own_head], 3)

    arrived(recv_two, 0)
    out_two, lse_two = None, None
    lanes_two = iota((256, 128), 1)
    for member in range(2):
        head = 2 * mine_two + member
        scores = matmul(masked(recv_two[0], DIM * member, DIM), recv_two[1], (1, 1)) * SCALE
        visible = seen(256, ROWS * block + shift_ref[0, head], RATE[0])
        scores = jnp.where(visible, scores, HIDDEN)
        scores_two[member] = scores
        top = jnp.max(scores, axis=1, keepdims=True)
        weights = jnp.exp(scores - top)
        total = jnp.sum(weights, axis=1, keepdims=True)
        out = matmul(weights.astype(BF16), recv_two[2], (1, 0)) / total
        lse = jnp.broadcast_to(top + jnp.log(total), (256, 128))
        out_two = out if member == 0 else jnp.where(lanes_two < DIM, out_two, out)
        lse_two = lse if member == 0 else jnp.where(lanes_two < 112, lse_two, lse)
    high, middle, low = three_parts(lse_two)
    turn = lanes_two % 16
    lse_two = jnp.where(turn == 0, high, jnp.where(turn == 1, middle, jnp.where(turn == 2, low, 0.0)))
    out_send_two[...] = jnp.where(lanes_two < 96, out_two, lse_two).astype(BF16)

    @pl.loop(1, 8)
    def _(step):
        other = (mine_two + step) % 8
        push(out_send_two.at[pl.ds(32 * other, 32)], out_recv_two.at[mine_two], 4, block + other)

    keep(out_send_two.at[pl.ds(32 * mine_two, 32)], out_recv_two.at[mine_two], 4)

    arrived(out_recv_three, 3)
    out_three = put_windows([out_recv_three[head] for head in range(HEADS)], DIM, 0)
    lse_three = put_windows([out_recv_three[head] for head in range(HEADS)], DIM, 64)
    spread(level_out.at[2], 1, out_three, False)
    spread(level_lse.at[2], 1, lse_three, False)
    arrived(out_recv_two, 4)
    row, column = iota((128, 128), 0), iota((128, 128), 1)
    widen = ((row >= 96) & (row < 99) & (column < DIM)) | (
        (row >= 112) & (row < 115) & (column >= DIM) & (column < 96)
    )
    widen = jnp.where(widen, 1.0, 0.0).astype(BF16)
    all_two = out_recv_two[...].reshape(256, 128)
    lse_all = matmul(all_two, widen, (1, 0)).reshape(8, 32, 128)
    out_all = all_two.astype(F32).reshape(8, 32, 128)
    spread(level_out.at[1], 0, put_windows([out_all[i] for i in range(8)], 96, 0), False)
    spread(level_lse.at[1], 0, put_windows([lse_all[i] for i in range(8)], 96, 0), False)
    for tile in range(TILES):
        levels = [level_lse[level, tile] for level in range(3)]
        best = jnp.maximum(jnp.maximum(levels[0], levels[1]), levels[2])
        mass = sum(jnp.exp(level - best) for level in levels)
        lse = best + jnp.log(mass)
        lse_wide[tile] = lse
        combined = jnp.zeros((ROWS, 128), F32)
        for level in range(3):
            share = jnp.exp(levels[level] - lse)
            combined = combined + jnp.where(share > 0, share * level_out[level, tile], 0.0)
        half, place = tile // 3, 128 * (tile % 3)
        att_halves[half, :, place : place + 128] = combined.astype(BF16)

    @pl.loop(1, 4)
    def _(step):
        other = (x + step) % 4
        push(att_halves.at[other % 2], att_all.at[x], 5, other * 32 + mine_three)

    keep(att_halves.at[x_low], att_all.at[x], 5)

    same_head = over_48(iota((HALF, HALF), 0)) == over_48(iota((HALF, HALF), 1))
    same_head = jnp.where(same_head, 1.0, 0.0).astype(BF16)
    for half in range(2):
        product = jnp.concatenate([source[3, 3 * half + tile] for tile in range(3)], axis=1)
        product = product * att_halves[half].astype(F32)
        high, middle, low = three_parts(product)
        summed = matmul(high.astype(BF16), same_head, (1, 0))
        summed = summed + matmul(middle.astype(BF16), same_head, (1, 0))
        for tile in range(3):
            delta_wide[3 * half + tile] = summed[:, 128 * tile : 128 * tile + 128]

    picked_lse, picked_delta = pick(lse_wide, 1), pick(delta_wide, 1)
    for head in range(HEADS):
        near = take_window(picked_lse, head * DIM, DIM, 0)
        far = take_window(picked_delta, head * DIM, DIM, 64)
        stat_send_three[head] = jnp.where(iota((8, 128), 1) < 64, near, far)
    picked_lse, picked_delta = pick(lse_wide, 0), pick(delta_wide, 0)
    coded = []
    for tile in range(TILES):
        columns = iota((32, 128), 1) + 128 * tile
        turn = (columns - DIM * over_48(columns)) >> 3
        value = jnp.zeros((32, 128), F32)
        pieces = three_parts(picked_lse[tile]) + three_parts(picked_delta[tile])
        for index, piece in enumerate(pieces):
            value = jnp.where(turn == index, piece, value)
        coded.append(value)
    for other in range(8):
        stat_send_two[other] = take_window(coded, 96 * other, 96, 0).astype(BF16)

    @pl.loop(1, 8)
    def _(step):
        other = (mine_two + step) % 8
        push(stat_send_two.at[other], stat_recv_two.at[pl.ds(32 * mine_two, 32)], 6, block + other)

    keep(stat_send_two.at[mine_two], stat_recv_two.at[pl.ds(32 * mine_two, 32)], 6)

    @pl.loop(0, HEADS)
    def _(step):
        head = (own_head + step) % HEADS
        other = worker(head)

        @pl.when(other != mine_three)
        def _():
            push(stat_send_three.at[head], stat_recv_three.at[mine_three], 7, plane + other)

    @pl.when(has_head)
    def _():
        keep(stat_send_three.at[own_head], stat_recv_three.at[mine_three], 7)

    attended = jnp.concatenate([att_halves[0], att_halves[1]], axis=1)
    mixed_ref[...] = matmul(attended, weight_ref[...], (1, 1)).astype(BF16)

    sums_q, sums_k, sums_v = ([None] * TILES for _ in range(3))
    for head in range(HEADS):
        lanes, first, span = window(head)
        place = slice(first, first + 1) if first < 128 else slice(first - 128, first - 127)
        lse = lse_wide[span[0]][:, place]
        delta = delta_wide[span[0]][:, place]
        grad = jnp.concatenate([source[3, tile] for tile in span], axis=1)
        grad_low = grad.astype(BF16)
        grad_head = part_of(grad, first)
        prob = jnp.exp(scores_one[head] - lse)
        dprob = matmul(grad_head, v_ref[:, lanes], (1, 1))
        dscore = (prob * (dprob - delta) * SCALE).astype(BF16)
        merge(sums_q, head, matmul(dscore, k_ref[:, lanes], (1, 0)), True)
        merge(sums_k, head, matmul(dscore, q_ref[:, lanes], (0, 0)), True)
        merge(sums_v, head, matmul(prob.astype(BF16), grad_low, (0, 0)), True)
    for tile in range(TILES):
        totals[0, tile] = sums_q[tile]
        totals[1, tile] = sums_k[tile]
        totals[2, tile] = sums_v[tile]

    @pl.when(has_head)
    def _():
        arrived(stat_recv_three, 7)
        first, second, first_turned, second_turned = split_three()
        stats = stat_recv_three[...].reshape(256, 128)
        prob = jnp.exp(scores_three[...] - stats[:, 0:1])
        dprob = matmul(part_of(second_turned, 0), second.astype(BF16), (1, 1))
        dscore = (prob * (dprob - stats[:, 64:65]) * SCALE).astype(BF16)
        grad_qk = matmul(dscore, part_of(first_turned, 0), (1, 0))
        grad_qk = grad_qk + matmul(dscore, part_of(first_turned, 64), (0, 0))
        grad_v = matmul(prob.astype(BF16), part_of(second_turned, 0), (0, 0))
        grads = jnp.concatenate([grad_qk.reshape(32, 8, 128), grad_v.reshape(32, 8, 128)], axis=1)
        grad_send_three[...] = grads.astype(BF16)

        @pl.loop(1, 32)
        def _(step):
            other = (mine_three + step) % 32
            push(grad_send_three.at[other], grad_recv_three.at[own_head], 8, plane + other)

        keep(grad_send_three.at[mine_three], grad_recv_three.at[own_head], 8)

    arrived(stat_recv_two, 6)
    row = iota((128, 256), 0)
    stats = stat_recv_two[...]
    grads = [None] * 3
    for member in range(2):

        def gathered(first):
            hit = (row == first) | (row == first + 8) | (row == first + 16)
            return matmul(stats, jnp.where(hit, 1.0, 0.0).astype(BF16), (1, 0))

        prob = jnp.exp(scores_two[member] - gathered(DIM * member))
        dprob = matmul(masked(recv_two[3], DIM * member, DIM), recv_two[2], (1, 1))
        dscore = (prob * (dprob - gathered(DIM * member + 24)) * SCALE).astype(BF16)
        news = (
            matmul(dscore, recv_two[1], (1, 0)),
            matmul(dscore, recv_two[0], (0, 0)),
            matmul(prob.astype(BF16), recv_two[3], (0, 0)),
        )
        for index, new in enumerate(news):
            old = grads[index]
            grads[index] = new if member == 0 else jnp.where(lanes_two < DIM, old, new)
    for index in range(3):
        grad_send_two[index] = grads[index].astype(BF16)

    @pl.loop(1, 8)
    def _(step):
        other = (mine_two + step) % 8
        push(grad_send_two.at[:, pl.ds(32 * other, 32)], grad_recv_two.at[mine_two], 9, block + other)

    keep(grad_send_two.at[:, pl.ds(32 * mine_two, 32)], grad_recv_two.at[mine_two], 9)

    arrived(cot_all, 2)
    arrived(att_all, 5)
    part[...] = matmul(
        cot_all[...].reshape(4 * ROWS, HALF), att_all[...].reshape(4 * ROWS, HALF), (0, 0)
    )
    for other in range(8):
        rows = jnp.concatenate(
            [part[24 * other : 24 * other + 24], part[192 + 24 * other : 216 + 24 * other]], axis=0
        )
        z_send[other] = rows.astype(BF16)

    @pl.loop(1, 8)
    def _(step):
        other = (z + step) % 8
        push(z_send.at[other], z_recv.at[z], 10, plane + 4 * other + y)

    keep(z_send.at[z], z_recv.at[z], 10)

    arrived(grad_recv_three, 8)
    received = grad_recv_three[...].astype(F32)
    for index, (place, rows) in enumerate(((0, slice(0, 8)), (64, slice(0, 8)), (0, slice(8, 16)))):
        tiles = put_windows([received[head, rows] for head in range(HEADS)], DIM, place)
        spread(totals.at[index], 1, tiles, True)
    arrived(grad_recv_two, 9)
    for index, out_ref in enumerate((dq_ref, dk_ref, dv_ref)):
        windows = [grad_recv_two[other, index].astype(F32) for other in range(8)]
        spread(totals.at[index], 0, put_windows(windows, 96, 0), True)
        for tile in range(TILES):
            out_ref[:, 128 * tile : 128 * tile + 128] = totals[index, tile].astype(BF16)

    arrived(z_recv, 10)
    rows = z_recv[0].astype(F32)
    for other in range(1, 8):
        rows = rows + z_recv[other].astype(F32)
    part[0:48] = rows
    for low in range(2):
        for other in range(4):
            start = 24 * low + 6 * other
            y_send[low, other, 0:6] = part[start : start + 6]
            y_send[low, other, 6:8] = jnp.zeros((2, HALF), F32)

    @pl.loop(1, 8)
    def _(step):
        other = (4 * x_low + y + step) % 8
        low, high = other // 4, other % 4
        device = (2 * x_high + low) * 32 + 4 * z + high
        push(y_send.at[low, high], y_recv.at[x_low, y], 11, device)

    keep(y_send.at[x_low, y], y_recv.at[x_low, y], 11)
    arrived(y_recv, 11)
    for low in range(2):
        rows = (y_recv[low, 0] + y_recv[low, 1]) + (y_recv[low, 2] + y_recv[low, 3])
        dw_ref[:, HALF * low : HALF * low + HALF] = rows[0:6] * (16384**-0.5)

    left(send_two.at[0:7], 0)
    left(cot_all.at[0:3], 2)
    left(out_send_two.at[0:224], 4)
    left(att_all.at[0:3], 5)
    left(stat_send_two.at[0:7], 6)
    left(grad_recv_two.at[0:7], 9)
    left(z_send.at[0:7], 10)
    left(y_send.at[0:1], 11)
    left(y_send.at[0, 0:3], 11)

    @pl.when(has_head)
    def _():
        left(send_three.at[0:15], 1)
        left(stat_send_three.at[0:15], 7)
        left(out_send_three.at[0:31], 3)
        left(grad_send_three.at[0:31], 8)

    @pl.when(jnp.logical_not(has_head))
    def _():
        left(send_three, 1)
        left(stat_send_three, 7)


def local(queries, keys, values, cotangent, out_weight, slide_lengths, head_dilation_shifts):
    vmem = pl.BlockSpec(memory_space=pltpu.VMEM)
    smem = pl.BlockSpec(memory_space=pltpu.SMEM)
    wide = jax.ShapeDtypeStruct((ROWS, WIDTH), BF16)
    scratch = [
        ((4, TILES, ROWS, 128), F32),
        ((8, 4, 32, 128), BF16),
        ((4, 256, 128), BF16),
        ((16, 16, 128), BF16),
        ((32, 16, 128), BF16),
        ((256, 128), BF16),
        ((8, 32, 128), BF16),
        ((32, 8, 128), F32),
        ((16, 8, 128), F32),
        ((8, 32, 128), BF16),
        ((256, 128), BF16),
        ((16, 8, 128), F32),
        ((32, 8, 128), F32),
        ((3, 256, 128), BF16),
        ((8, 3, 32, 128), BF16),
        ((32, 16, 128), BF16),
        ((16, 16, 128), BF16),
        ((2, ROWS, HALF), BF16),
        ((2, ROWS, HALF), BF16),
        ((4, ROWS, HALF), BF16),
        ((4, ROWS, HALF), BF16),
        ((HALF, HALF), F32),
        ((8, 48, HALF), BF16),
        ((8, 48, HALF), BF16),
        ((2, 4, 8, HALF), F32),
        ((2, 4, 8, HALF), F32),
        ((HEADS, ROWS, ROWS), F32),
        ((2, 256, 256), F32),
        ((256, 256), F32),
        ((3, TILES, ROWS, 128), F32),
        ((3, TILES, ROWS, 128), F32),
        ((TILES, ROWS, 128), F32),
        ((TILES, ROWS, 128), F32),
        ((3, TILES, ROWS, 128), F32),
    ]
    return pl.pallas_call(
        kernel,
        out_shape=(wide, wide, wide, wide, jax.ShapeDtypeStruct((WIDTH // 128, WIDTH), F32)),
        in_specs=[vmem] * 5 + [smem] * 2,
        out_specs=(vmem,) * 5,
        scratch_shapes=[pltpu.VMEM(shape, dtype) for shape, dtype in scratch]
        + [pltpu.SemaphoreType.DMA((12,)), pltpu.SemaphoreType.DMA((12,))],
        compiler_params=pltpu.CompilerParams(
            collective_id=0, has_side_effects=True, vmem_limit_bytes=48 * 1024 * 1024
        ),
        name="dilated_attention",
    )(queries, keys, values, cotangent, out_weight, slide_lengths, head_dilation_shifts)


def solution(mesh):
    rows = P(("dp", "seq"), None)
    return jax.shard_map(
        local,
        mesh=mesh,
        in_specs=(rows, rows, rows, rows, P(), P("dp"), P()),
        out_specs=(rows,) * 5,
        check_vma=False,
    )
```

```python
import jax
import jax.numpy as jnp
from jax import lax
from jax.experimental import pallas as pl
from jax.experimental.pallas import tpu as pltpu
from jax.sharding import PartitionSpec as P

HEADS = 16
DIM = 48
WIDTH = HEADS * DIM
ROWS = 128
TILES = WIDTH // 128
HALF = WIDTH // 2
RATE = (4, 16)
COUNT = (ROWS // 4, ROWS // 16)
SCALE = DIM**-0.5
HIDDEN = -1e30
EARLY = 8
VMEM = 60 * 1024 * 1024
F32 = jnp.float32
BF16 = jnp.bfloat16
MESH = pl.DeviceIdType.MESH


def matmul(a, b, contract):
    return lax.dot_general(a, b, ((contract[:1], contract[1:]), ((), ())), preferred_element_type=F32)


def iota(shape, axis):
    return lax.broadcasted_iota(jnp.int32, shape, axis)


def over_48(columns):
    return (columns * 1366) >> 16


def tile_span(first, width):
    return range(first // 128, (first + width - 1) // 128 + 1)


def take_window(tiles, first, width, place):
    at, off = first // 128, first % 128
    turn = (place - off) % 128
    near = tiles[at] if turn == 0 else pltpu.roll(tiles[at], turn, 1)
    if off + width <= 128:
        return near
    far = tiles[at + 1] if turn == 0 else pltpu.roll(tiles[at + 1], turn, 1)
    return jnp.where(iota(near.shape, 1) < place + 128 - off, near, far)


def put_windows(windows, width, place):
    tiles = [None] * TILES
    for index, window in enumerate(windows):
        first = index * width
        off = first % 128
        turn = (off - place) % 128
        turned = window if turn == 0 else pltpu.roll(window, turn, 1)
        for tile in tile_span(first, width):
            if tiles[tile] is None:
                tiles[tile] = turned
            else:
                columns = iota(window.shape, 1) + 128 * tile
                inside = (columns >= first) & (columns < first + width)
                tiles[tile] = jnp.where(inside, turned, tiles[tile])
    return tiles


def three_parts(value):
    high = value.astype(BF16).astype(F32)
    rest = value - high
    middle = rest.astype(BF16).astype(F32)
    return high, middle, rest - middle


def kernel(
    q_far,
    k_far,
    v_far,
    cot_far,
    weight_far,
    length_far,
    shift_far,
    mixed_far,
    dq_far,
    dk_far,
    dv_far,
    dw_far,
    mixed_ref,
    dq_ref,
    dk_ref,
    dv_ref,
    dw_ref,
    q_ref,
    k_ref,
    v_ref,
    cot_ref,
    weight_ref,
    length_ref,
    shift_ref,
    source,
    send_two,
    recv_two,
    d_send_two,
    d_recv_two,
    send_three,
    recv_three,
    out_send_two,
    out_recv_two,
    out_send_three,
    out_recv_three,
    stat_send_two,
    stat_recv_two,
    stat_send_three,
    stat_recv_three,
    grad_send_two,
    grad_recv_two,
    grad_send_three,
    grad_recv_three,
    cot_halves,
    att_halves,
    cot_all,
    att_all,
    part,
    z_send,
    z_recv,
    y_send,
    y_recv,
    scores_one,
    scores_two,
    scores_three,
    level_out,
    level_lse,
    lse_wide,
    delta_wide,
    totals,
    send_sems,
    recv_sems,
    in_sems,
    out_sems,
):
    pairs = (
        (shift_far, shift_ref),
        (q_far, q_ref),
        (k_far, k_ref),
        (v_far, v_ref),
        (cot_far, cot_ref),
        (weight_far, weight_ref),
        (length_far, length_ref),
    )
    incoming = [pltpu.make_async_copy(*pair, in_sems.at[index]) for index, pair in enumerate(pairs)]
    for copy in incoming:
        copy.start()
    pairs = (
        (mixed_ref, mixed_far),
        (dq_ref, dq_far),
        (dk_ref, dk_far),
        (dv_ref, dv_far),
        (dw_ref, dw_far),
    )
    outgoing = [pltpu.make_async_copy(*pair, out_sems.at[index]) for index, pair in enumerate(pairs)]

    rank = lax.axis_index("seq")
    x, z, y = rank // 32, (rank % 32) // 4, rank % 4
    x_high, x_low = x // 2, x % 2
    plane, mine_three = rank - rank % 32, rank % 32
    block, mine_two = rank - rank % 8, rank % 8
    has_head = mine_three % 2 == (mine_three // 4) % 2
    own_head = mine_three // 2

    def worker(head):
        return 2 * head + (head // 2) % 2

    barrier = pltpu.get_barrier_semaphore()

    def greet(device):
        pl.semaphore_signal(barrier, inc=1, device_id={"seq": device}, device_id_type=MESH)

    @pl.loop(1, 32)
    def _(step):
        greet(plane + (mine_three + step) % 32)

    @pl.loop(1, 4)
    def _(step):
        greet(((x + step) % 4) * 32 + mine_three)

    other_x = 2 * x_high + 1 - x_low

    @pl.loop(1, 4)
    def _(step):
        greet(other_x * 32 + z * 4 + (y + step) % 4)

    def push(from_ref, to_ref, index, device):
        pltpu.make_async_remote_copy(
            src_ref=from_ref,
            dst_ref=to_ref,
            send_sem=send_sems.at[index],
            recv_sem=recv_sems.at[index],
            device_id={"seq": device},
            device_id_type=MESH,
        ).start()

    def keep(from_ref, to_ref, index):
        pltpu.make_async_copy(from_ref, to_ref, recv_sems.at[index]).start()

    def arrived(ref, index):
        pltpu.make_async_copy(ref, ref, recv_sems.at[index]).wait()

    def left(ref, index):
        pltpu.make_async_copy(ref, ref, send_sems.at[index]).wait()

    for index in range(4):
        incoming[index].wait()
    for index, ref in enumerate((q_ref, k_ref, v_ref)):
        for tile in range(TILES):
            source[index, tile] = ref[:, 128 * tile : 128 * tile + 128].astype(F32)

    def column_shift(level, tile):
        shape = (COUNT[level], 128)
        heads = over_48(iota(shape, 1) + 128 * tile)
        value = jnp.zeros(shape, jnp.int32)
        for head in range(HEADS):
            if tile in tile_span(head * DIM, DIM):
                value = jnp.where(heads == head, shift_ref[level, head], value)
        return value

    shifts = [[column_shift(level, tile) for tile in range(TILES)] for level in range(2)]

    def pick(view, level):
        tiles = []
        for tile in range(TILES):
            value = view[tile, pl.ds(0, COUNT[level], RATE[level]), :]
            for offset in range(1, RATE[level]):
                rows = view[tile, pl.ds(offset, COUNT[level], RATE[level]), :]
                value = jnp.where(shifts[level][tile] == offset, rows, value)
            tiles.append(value)
        return tiles

    def spread(view, level, tiles, add):
        for tile in range(TILES):
            for offset in range(RATE[level]):
                place = (tile, pl.ds(offset, COUNT[level], RATE[level]), slice(None))
                other = view[place] if add else HIDDEN
                value = tiles[tile] + other if add else tiles[tile]
                view[place] = jnp.where(shifts[level][tile] == offset, value, other)

    picked_three = [pick(source.at[index], 1) for index in range(3)]
    for head in range(HEADS):
        low = iota((8, 128), 1) < 64
        near = take_window(picked_three[0], head * DIM, DIM, 0)
        far = take_window(picked_three[1], head * DIM, DIM, 64)
        totals[0, 0, 0:8] = jnp.where(low, near, far)
        totals[0, 0, 8:16] = take_window(picked_three[2], head * DIM, DIM, 0)
        send_three[head] = totals[0, 0, 0:16].astype(BF16)

    pl.semaphore_wait(barrier, 37)

    @pl.loop(0, HEADS)
    def _(step):
        head = (own_head + step) % HEADS
        other = worker(head)

        @pl.when(other != mine_three)
        def _():
            push(send_three.at[head], recv_three.at[mine_three], 1, plane + other)

    @pl.when(has_head)
    def _():
        keep(send_three.at[own_head], recv_three.at[mine_three], 1)

    for index in range(3):
        picked = pick(source.at[index], 0)
        for other in range(8):
            send_two[other, index] = take_window(picked, 96 * other, 96, 0).astype(BF16)

    @pl.loop(1, 8)
    def _(step):
        other = (mine_two + step) % 8
        push(send_two.at[other], recv_two.at[:, pl.ds(32 * mine_two, 32)], 0, block + other)

    keep(send_two.at[mine_two], recv_two.at[:, pl.ds(32 * mine_two, 32)], 0)

    for index in range(4, 7):
        incoming[index].wait()
    cot_halves[0] = cot_ref[:, :HALF]
    cot_halves[1] = cot_ref[:, HALF:]

    @pl.loop(1, 4)
    def _(step):
        other = (x + step) % 4
        push(cot_halves.at[other // 2], cot_all.at[x], 2, other * 32 + mine_three)

    keep(cot_halves.at[x_high], cot_all.at[x], 2)
    d_attended = jnp.dot(cot_ref[...], weight_ref[...], preferred_element_type=F32).astype(BF16)
    for tile in range(TILES):
        source[3, tile] = d_attended[:, 128 * tile : 128 * tile + 128].astype(F32)
    picked = pick(source.at[3], 0)
    for other in range(8):
        d_send_two[other] = take_window(picked, 96 * other, 96, 0).astype(BF16)

    @pl.loop(1, 8)
    def _(step):
        other = (mine_two + step) % 8
        push(d_send_two.at[other], d_recv_two.at[pl.ds(32 * mine_two, 32)], 12, block + other)

    keep(d_send_two.at[mine_two], d_recv_two.at[pl.ds(32 * mine_two, 32)], 12)

    ends = []
    running = 0
    for index in range(8):
        running = running + length_ref[index]
        ends.append(running)

    def slide(positions):
        value = jnp.zeros(positions.shape, jnp.int32)
        for end in ends:
            value = value + jnp.where(positions >= end, 1, 0)
        return value

    def seen(count, first, stride):
        rows = slide(first + stride * iota((count, 128), 0))
        columns = slide(first + stride * iota((8, count), 1))[0:1]
        rows = jnp.concatenate([rows] * (count // 128), axis=1)
        return rows == jnp.broadcast_to(columns, (count, count))

    def lane_mask(shape, first, width):
        lanes = iota(shape, 1)
        return (lanes >= first) & (lanes < first + width)

    def masked(value, first, width):
        inside = lane_mask(value.shape, first, width)
        return jnp.where(inside, value.astype(F32), 0.0).astype(BF16)

    def window(head):
        span = tile_span(head * DIM, DIM)
        return slice(128 * span[0], 128 * (span[-1] + 1)), head * DIM - 128 * span[0], span

    visible_one = seen(ROWS, ROWS * rank, 1)
    outs, tops, sums = ([None] * TILES for _ in range(3))

    def merge(tiles, head, value, wide):
        _, first, span = window(head)
        for index, tile in enumerate(span):
            piece = value[:, 128 * index : 128 * index + 128] if wide else value
            piece = jnp.broadcast_to(piece, (ROWS, 128))
            if tiles[tile] is None:
                tiles[tile] = piece
            else:
                columns = iota((ROWS, 128), 1) + 128 * index
                inside = (columns >= first) & (columns < first + DIM)
                tiles[tile] = jnp.where(inside, piece, tiles[tile])

    for head in range(HEADS):
        lanes, first, span = window(head)
        scores = matmul(masked(q_ref[:, lanes], first, DIM), k_ref[:, lanes], (1, 1)) * SCALE
        scores = jnp.where(visible_one, scores, HIDDEN)
        scores_one[head] = scores
        top = jnp.max(scores, axis=1, keepdims=True)
        weights = jnp.exp(scores - top)
        total = jnp.sum(weights, axis=1, keepdims=True)
        out = matmul(weights.astype(BF16), v_ref[:, lanes], (1, 0))
        merge(outs, head, out, True)
        merge(tops, head, top, False)
        merge(sums, head, total, False)
    for tile in range(TILES):
        level_out[0, tile] = outs[tile] / sums[tile]
        level_lse[0, tile] = tops[tile] + jnp.log(sums[tile])

    def split_three():
        both = recv_three[...].astype(F32).reshape(32, 2, 8, 128)
        first = both[:, 0].reshape(256, 128)
        return first, pltpu.roll(first, 64, 1), both[:, 1].reshape(256, 128).astype(BF16)

    def part_of(value, first):
        return jnp.where(lane_mask(value.shape, first, DIM), value, 0.0).astype(BF16)

    @pl.when(has_head)
    def _():
        arrived(recv_three, 1)
        first, turned, value_rows = split_three()
        scores = matmul(part_of(first, 0), turned.astype(BF16), (1, 1)) * SCALE
        visible = seen(256, 4096 * x + shift_ref[1, own_head], RATE[1])
        scores = jnp.where(visible, scores, HIDDEN)
        scores_three[...] = scores
        top = jnp.max(scores, axis=1, keepdims=True)
        weights = jnp.exp(scores - top)
        total = jnp.sum(weights, axis=1, keepdims=True)
        out = matmul(weights.astype(BF16), value_rows, (1, 0)) / total
        lse = jnp.broadcast_to(top + jnp.log(total), (256, 128))
        out = jnp.where(iota((256, 128), 1) < 64, out, lse)
        out_send_three[...] = out.reshape(32, 8, 128)

        @pl.loop(1, 32)
        def _(step):
            other = (mine_three + step) % 32
            push(out_send_three.at[other], out_recv_three.at[own_head], 3, plane + other)

        keep(out_send_three.at[mine_three], out_recv_three.at[own_head], 3)

    arrived(recv_two, 0)
    out_two, lse_two = None, None
    lanes_two = iota((256, 128), 1)
    for member in range(2):
        head = 2 * mine_two + member
        scores = matmul(masked(recv_two[0], DIM * member, DIM), recv_two[1], (1, 1)) * SCALE
        visible = seen(256, ROWS * block + shift_ref[0, head], RATE[0])
        scores = jnp.where(visible, scores, HIDDEN)
        scores_two[member] = scores
        top = jnp.max(scores, axis=1, keepdims=True)
        weights = jnp.exp(scores - top)
        total = jnp.sum(weights, axis=1, keepdims=True)
        out = matmul(weights.astype(BF16), recv_two[2], (1, 0)) / total
        lse = jnp.broadcast_to(top + jnp.log(total), (256, 128))
        out_two = out if member == 0 else jnp.where(lanes_two < DIM, out_two, out)
        lse_two = lse if member == 0 else jnp.where(lanes_two < 112, lse_two, lse)
    high, middle, low = three_parts(lse_two)
    turn = lanes_two % 16
    lse_two = jnp.where(turn == 0, high, jnp.where(turn == 1, middle, jnp.where(turn == 2, low, 0.0)))
    out_send_two[...] = jnp.where(lanes_two < 96, out_two, lse_two).astype(BF16)

    @pl.loop(1, 8)
    def _(step):
        other = (mine_two + step) % 8
        push(out_send_two.at[pl.ds(32 * other, 32)], out_recv_two.at[mine_two], 4, block + other)

    keep(out_send_two.at[pl.ds(32 * mine_two, 32)], out_recv_two.at[mine_two], 4)

    arrived(out_recv_three, 3)
    out_three = put_windows([out_recv_three[head] for head in range(HEADS)], DIM, 0)
    lse_three = put_windows([out_recv_three[head] for head in range(HEADS)], DIM, 64)
    spread(level_out.at[2], 1, out_three, False)
    spread(level_lse.at[2], 1, lse_three, False)
    arrived(out_recv_two, 4)
    row, column = iota((128, 128), 0), iota((128, 128), 1)
    widen = ((row >= 96) & (row < 99) & (column < DIM)) | (
        (row >= 112) & (row < 115) & (column >= DIM) & (column < 96)
    )
    widen = jnp.where(widen, 1.0, 0.0).astype(BF16)
    all_two = out_recv_two[...].reshape(256, 128)
    lse_all = matmul(all_two, widen, (1, 0)).reshape(8, 32, 128)
    out_all = all_two.astype(F32).reshape(8, 32, 128)
    spread(level_out.at[1], 0, put_windows([out_all[i] for i in range(8)], 96, 0), False)
    spread(level_lse.at[1], 0, put_windows([lse_all[i] for i in range(8)], 96, 0), False)
    for tile in range(TILES):
        levels = [level_lse[level, tile] for level in range(3)]
        best = jnp.maximum(jnp.maximum(levels[0], levels[1]), levels[2])
        mass = sum(jnp.exp(level - best) for level in levels)
        lse = best + jnp.log(mass)
        lse_wide[tile] = lse
        combined = jnp.zeros((ROWS, 128), F32)
        for level in range(3):
            share = jnp.exp(levels[level] - lse)
            combined = combined + jnp.where(share > 0, share * level_out[level, tile], 0.0)
        half, place = tile // 3, 128 * (tile % 3)
        att_halves[half, :, place : place + 128] = combined.astype(BF16)

    @pl.loop(1, 4)
    def _(step):
        other = (x + step) % 4
        push(att_halves.at[other % 2], att_all.at[x], 5, other * 32 + mine_three)

    keep(att_halves.at[x_low], att_all.at[x], 5)

    same_head = over_48(iota((HALF, HALF), 0)) == over_48(iota((HALF, HALF), 1))
    same_head = jnp.where(same_head, 1.0, 0.0).astype(BF16)
    for half in range(2):
        product = jnp.concatenate([source[3, 3 * half + tile] for tile in range(3)], axis=1)
        product = product * att_halves[half].astype(F32)
        high, middle, low = three_parts(product)
        summed = matmul(high.astype(BF16), same_head, (1, 0))
        summed = summed + matmul(middle.astype(BF16), same_head, (1, 0))
        for tile in range(3):
            delta_wide[3 * half + tile] = summed[:, 128 * tile : 128 * tile + 128]

    picked_lse, picked_delta = pick(lse_wide, 1), pick(delta_wide, 1)
    picked_grad = pick(source.at[3], 1)
    lanes = iota((8, 128), 1)
    for head in range(HEADS):
        near = take_window(picked_lse, head * DIM, DIM, 0)
        middle = take_window(picked_delta, head * DIM, DIM, 32)
        far = take_window(picked_grad, head * DIM, DIM, 64)
        stat_send_three[head] = jnp.where(lanes < 32, near, jnp.where(lanes < 64, middle, far))
    picked_lse, picked_delta = pick(lse_wide, 0), pick(delta_wide, 0)
    coded = []
    for tile in range(TILES):
        columns = iota((32, 128), 1) + 128 * tile
        turn = (columns - DIM * over_48(columns)) >> 3
        value = jnp.zeros((32, 128), F32)
        pieces = three_parts(picked_lse[tile]) + three_parts(picked_delta[tile])
        for index, piece in enumerate(pieces):
            value = jnp.where(turn == index, piece, value)
        coded.append(value)
    for other in range(8):
        stat_send_two[other] = take_window(coded, 96 * other, 96, 0).astype(BF16)

    @pl.loop(1, 8)
    def _(step):
        other = (mine_two + step) % 8
        push(stat_send_two.at[other], stat_recv_two.at[pl.ds(32 * mine_two, 32)], 6, block + other)

    keep(stat_send_two.at[mine_two], stat_recv_two.at[pl.ds(32 * mine_two, 32)], 6)

    @pl.loop(0, HEADS)
    def _(step):
        head = (own_head + step) % HEADS
        other = worker(head)

        @pl.when(other != mine_three)
        def _():
            push(stat_send_three.at[head], stat_recv_three.at[mine_three], 7, plane + other)

    @pl.when(has_head)
    def _():
        keep(stat_send_three.at[own_head], stat_recv_three.at[mine_three], 7)

    attended = jnp.concatenate([att_halves[0], att_halves[1]], axis=1)
    mixed_ref[...] = matmul(attended, weight_ref[...], (1, 1)).astype(BF16)
    outgoing[0].start()

    sums_q, sums_k, sums_v = ([None] * TILES for _ in range(3))
    def one_back(head):
        lanes, first, span = window(head)
        place = slice(first, first + 1) if first < 128 else slice(first - 128, first - 127)
        lse = lse_wide[span[0]][:, place]
        delta = delta_wide[span[0]][:, place]
        grad = jnp.concatenate([source[3, tile] for tile in span], axis=1)
        grad_low = grad.astype(BF16)
        grad_head = part_of(grad, first)
        prob = jnp.exp(scores_one[head] - lse)
        dprob = matmul(grad_head, v_ref[:, lanes], (1, 1))
        dscore = (prob * (dprob - delta) * SCALE).astype(BF16)
        merge(sums_q, head, matmul(dscore, k_ref[:, lanes], (1, 0)), True)
        merge(sums_k, head, matmul(dscore, q_ref[:, lanes], (0, 0)), True)
        merge(sums_v, head, matmul(prob.astype(BF16), grad_low, (0, 0)), True)

    for head in range(EARLY):
        one_back(head)

    arrived(cot_all, 2)
    arrived(att_all, 5)
    part[...] = matmul(
        cot_all[...].reshape(4 * ROWS, HALF), att_all[...].reshape(4 * ROWS, HALF), (0, 0)
    )
    for other in range(8):
        rows = jnp.concatenate(
            [part[24 * other : 24 * other + 24], part[192 + 24 * other : 216 + 24 * other]], axis=0
        )
        z_send[other] = rows.astype(BF16)

    @pl.loop(1, 8)
    def _(step):
        other = (z + step) % 8
        push(z_send.at[other], z_recv.at[z], 10, plane + 4 * other + y)

    keep(z_send.at[z], z_recv.at[z], 10)

    @pl.when(has_head)
    def _():
        arrived(stat_recv_three, 7)
        first, turned, value_rows = split_three()
        stats = stat_recv_three[...].reshape(256, 128)
        grad_rows = part_of(pltpu.roll(stats, 64, 1), 0)
        prob = jnp.exp(scores_three[...] - stats[:, 0:1])
        dprob = matmul(grad_rows, value_rows, (1, 1))
        dscore = (prob * (dprob - stats[:, 32:33]) * SCALE).astype(BF16)
        grad_qk = matmul(dscore, part_of(turned, 0), (1, 0))
        grad_qk = grad_qk + matmul(dscore, part_of(turned, 64), (0, 0))
        grad_v = matmul(prob.astype(BF16), grad_rows, (0, 0))
        grads = jnp.concatenate([grad_qk.reshape(32, 8, 128), grad_v.reshape(32, 8, 128)], axis=1)
        grad_send_three[...] = grads.astype(BF16)

        @pl.loop(1, 32)
        def _(step):
            other = (mine_three + step) % 32
            push(grad_send_three.at[other], grad_recv_three.at[own_head], 8, plane + other)

        keep(grad_send_three.at[mine_three], grad_recv_three.at[own_head], 8)

    arrived(d_recv_two, 12)
    arrived(stat_recv_two, 6)
    row = iota((128, 256), 0)
    stats = stat_recv_two[...]
    grads = [None] * 3
    for member in range(2):

        def gathered(first):
            hit = (row == first) | (row == first + 8) | (row == first + 16)
            return matmul(stats, jnp.where(hit, 1.0, 0.0).astype(BF16), (1, 0))

        prob = jnp.exp(scores_two[member] - gathered(DIM * member))
        dprob = matmul(masked(d_recv_two[...], DIM * member, DIM), recv_two[2], (1, 1))
        dscore = (prob * (dprob - gathered(DIM * member + 24)) * SCALE).astype(BF16)
        news = (
            matmul(dscore, recv_two[1], (1, 0)),
            matmul(dscore, recv_two[0], (0, 0)),
            matmul(prob.astype(BF16), d_recv_two[...], (0, 0)),
        )
        for index, new in enumerate(news):
            old = grads[index]
            grads[index] = new if member == 0 else jnp.where(lanes_two < DIM, old, new)
    for index in range(3):
        grad_send_two[index] = grads[index].astype(BF16)

    @pl.loop(1, 8)
    def _(step):
        other = (mine_two + step) % 8
        push(grad_send_two.at[:, pl.ds(32 * other, 32)], grad_recv_two.at[mine_two], 9, block + other)

    keep(grad_send_two.at[:, pl.ds(32 * mine_two, 32)], grad_recv_two.at[mine_two], 9)

    for head in range(EARLY, HEADS):
        one_back(head)
    for tile in range(TILES):
        totals[0, tile] = sums_q[tile]
        totals[1, tile] = sums_k[tile]
        totals[2, tile] = sums_v[tile]

    arrived(z_recv, 10)
    rows = z_recv[0].astype(F32)
    for other in range(1, 8):
        rows = rows + z_recv[other].astype(F32)
    part[0:48] = rows
    for low in range(2):
        for other in range(4):
            start = 24 * low + 6 * other
            y_send[low, other, 0:6] = part[start : start + 6]
            y_send[low, other, 6:8] = jnp.zeros((2, HALF), F32)

    @pl.loop(1, 8)
    def _(step):
        other = (4 * x_low + y + step) % 8
        low, high = other // 4, other % 4
        device = (2 * x_high + low) * 32 + 4 * z + high
        push(y_send.at[low, high], y_recv.at[x_low, y], 11, device)

    keep(y_send.at[x_low, y], y_recv.at[x_low, y], 11)

    arrived(grad_recv_three, 8)
    received = grad_recv_three[...].astype(F32)
    for index, (place, rows) in enumerate(((0, slice(0, 8)), (64, slice(0, 8)), (0, slice(8, 16)))):
        tiles = put_windows([received[head, rows] for head in range(HEADS)], DIM, place)
        spread(totals.at[index], 1, tiles, True)
    arrived(grad_recv_two, 9)
    for index, out_ref in enumerate((dq_ref, dk_ref, dv_ref)):
        windows = [grad_recv_two[other, index].astype(F32) for other in range(8)]
        spread(totals.at[index], 0, put_windows(windows, 96, 0), True)
        for tile in range(TILES):
            out_ref[:, 128 * tile : 128 * tile + 128] = totals[index, tile].astype(BF16)
        outgoing[1 + index].start()

    arrived(y_recv, 11)
    for low in range(2):
        rows = (y_recv[low, 0] + y_recv[low, 1]) + (y_recv[low, 2] + y_recv[low, 3])
        dw_ref[:, HALF * low : HALF * low + HALF] = rows[0:6] * (16384**-0.5)
    outgoing[4].start()

    left(send_two.at[0:7], 0)
    left(cot_all.at[0:3], 2)
    left(out_send_two.at[0:224], 4)
    left(att_all.at[0:3], 5)
    left(stat_send_two.at[0:7], 6)
    left(grad_recv_two.at[0:7], 9)
    left(z_send.at[0:7], 10)
    left(d_send_two.at[0:7], 12)
    left(y_send.at[0:1], 11)
    left(y_send.at[0, 0:3], 11)

    @pl.when(has_head)
    def _():
        left(send_three.at[0:15], 1)
        left(stat_send_three.at[0:15], 7)
        left(out_send_three.at[0:31], 3)
        left(grad_send_three.at[0:31], 8)

    @pl.when(jnp.logical_not(has_head))
    def _():
        left(send_three, 1)
        left(stat_send_three, 7)

    for copy in outgoing:
        copy.wait()


def finish(*refs):
    sources, results, holders, sems = refs[:5], refs[5:10], refs[10:15], refs[15]
    inward, outward = [], []
    for index in range(5):
        inward.append(pltpu.make_async_copy(sources[index], holders[index], sems.at[0, index]))
        outward.append(pltpu.make_async_copy(holders[index], results[index], sems.at[1, index]))
        inward[index].start()
    for index in range(5):
        inward[index].wait()
        outward[index].start()
    for index in range(5):
        outward[index].wait()


def local(queries, keys, values, cotangent, out_weight, slide_lengths, head_dilation_shifts):
    far = pl.BlockSpec(memory_space=pltpu.HBM)
    wide = jax.ShapeDtypeStruct((ROWS, WIDTH), BF16)
    scratch = [
        ((4, TILES, ROWS, 128), F32),
        ((8, 3, 32, 128), BF16),
        ((3, 256, 128), BF16),
        ((8, 32, 128), BF16),
        ((256, 128), BF16),
        ((16, 16, 128), BF16),
        ((32, 16, 128), BF16),
        ((256, 128), BF16),
        ((8, 32, 128), BF16),
        ((32, 8, 128), F32),
        ((16, 8, 128), F32),
        ((8, 32, 128), BF16),
        ((256, 128), BF16),
        ((16, 8, 128), F32),
        ((32, 8, 128), F32),
        ((3, 256, 128), BF16),
        ((8, 3, 32, 128), BF16),
        ((32, 16, 128), BF16),
        ((16, 16, 128), BF16),
        ((2, ROWS, HALF), BF16),
        ((2, ROWS, HALF), BF16),
        ((4, ROWS, HALF), BF16),
        ((4, ROWS, HALF), BF16),
        ((HALF, HALF), F32),
        ((8, 48, HALF), BF16),
        ((8, 48, HALF), BF16),
        ((2, 4, 8, HALF), F32),
        ((2, 4, 8, HALF), F32),
        ((HEADS, ROWS, ROWS), F32),
        ((2, 256, 256), F32),
        ((256, 256), F32),
        ((3, TILES, ROWS, 128), F32),
        ((3, TILES, ROWS, 128), F32),
        ((TILES, ROWS, 128), F32),
        ((TILES, ROWS, 128), F32),
        ((3, TILES, ROWS, 128), F32),
    ]
    out_shape = (wide, wide, wide, wide, jax.ShapeDtypeStruct((WIDTH // 128, WIDTH), F32))
    results = pl.pallas_call(
        kernel,
        out_shape=out_shape,
        in_specs=[far] * 7,
        out_specs=(far,) * 5,
        scratch_shapes=[pltpu.VMEM((ROWS, WIDTH), BF16)] * 4
        + [pltpu.VMEM((WIDTH // 128, WIDTH), F32)]
        + [pltpu.VMEM((ROWS, WIDTH), BF16)] * 4
        + [pltpu.VMEM((WIDTH, WIDTH), BF16), pltpu.SMEM((8,), jnp.int32), pltpu.SMEM((2, HEADS), jnp.int32)]
        + [pltpu.VMEM(shape, dtype) for shape, dtype in scratch]
        + [pltpu.SemaphoreType.DMA((13,)), pltpu.SemaphoreType.DMA((13,)), pltpu.SemaphoreType.DMA((7,)), pltpu.SemaphoreType.DMA((5,))],
        compiler_params=pltpu.CompilerParams(
            collective_id=0, has_side_effects=True, vmem_limit_bytes=VMEM
        ),
        name="dilated_attention",
    )(queries, keys, values, cotangent, out_weight, slide_lengths, head_dilation_shifts)
    return pl.pallas_call(
        finish,
        out_shape=out_shape,
        in_specs=[far] * 5,
        out_specs=(far,) * 5,
        scratch_shapes=[pltpu.VMEM(shape.shape, shape.dtype) for shape in out_shape]
        + [pltpu.SemaphoreType.DMA((2, 5))],
        compiler_params=pltpu.CompilerParams(vmem_limit_bytes=VMEM),
        name="results_to_hbm",
    )(*results)


def solution(mesh):
    rows = P(("dp", "seq"), None)
    return jax.shard_map(
        local,
        mesh=mesh,
        in_specs=(rows, rows, rows, rows, P(), P("dp"), P()),
        out_specs=(rows,) * 5,
        check_vma=False,
    )
```

```python
import jax
import jax.numpy as jnp
from jax import lax
from jax.experimental import pallas as pl
from jax.experimental.pallas import tpu as pltpu
from jax.sharding import PartitionSpec as P

HEADS = 16
DIM = 48
WIDTH = HEADS * DIM
ROWS = 128
TILES = WIDTH // 128
HALF = WIDTH // 2
RATE = (4, 16)
COUNT = (ROWS // 4, ROWS // 16)
SCALE = DIM**-0.5
HIDDEN = -1e30
EARLY = (0, 2, 4, 6)
VMEM = 60 * 1024 * 1024
F32 = jnp.float32
BF16 = jnp.bfloat16
MESH = pl.DeviceIdType.MESH


def matmul(a, b, contract):
    return lax.dot_general(a, b, ((contract[:1], contract[1:]), ((), ())), preferred_element_type=F32)


def iota(shape, axis):
    return lax.broadcasted_iota(jnp.int32, shape, axis)


def over_48(columns):
    return (columns * 1366) >> 16


def tile_span(first, width):
    return range(first // 128, (first + width - 1) // 128 + 1)


def take_window(tiles, first, width, place):
    at, off = first // 128, first % 128
    turn = (place - off) % 128
    near = tiles[at] if turn == 0 else pltpu.roll(tiles[at], turn, 1)
    if off + width <= 128:
        return near
    far = tiles[at + 1] if turn == 0 else pltpu.roll(tiles[at + 1], turn, 1)
    return jnp.where(iota(near.shape, 1) < place + 128 - off, near, far)


def put_windows(windows, width, place):
    tiles = [None] * TILES
    for index, window in enumerate(windows):
        first = index * width
        off = first % 128
        turn = (off - place) % 128
        turned = window if turn == 0 else pltpu.roll(window, turn, 1)
        for tile in tile_span(first, width):
            if tiles[tile] is None:
                tiles[tile] = turned
            else:
                columns = iota(window.shape, 1) + 128 * tile
                inside = (columns >= first) & (columns < first + width)
                tiles[tile] = jnp.where(inside, turned, tiles[tile])
    return tiles


def three_parts(value):
    high = value.astype(BF16).astype(F32)
    rest = value - high
    middle = rest.astype(BF16).astype(F32)
    return high, middle, rest - middle


def kernel(
    q_far,
    k_far,
    v_far,
    cot_far,
    weight_far,
    length_far,
    shift_far,
    mixed_far,
    dq_far,
    dk_far,
    dv_far,
    dw_far,
    mixed_ref,
    dq_ref,
    dk_ref,
    dv_ref,
    dw_ref,
    q_ref,
    k_ref,
    v_ref,
    cot_ref,
    weight_ref,
    length_ref,
    shift_ref,
    source,
    send_two,
    recv_two,
    d_send_two,
    d_recv_two,
    send_three,
    recv_three,
    out_send_two,
    out_recv_two,
    out_send_three,
    out_recv_three,
    stat_send_two,
    stat_recv_two,
    stat_send_three,
    stat_recv_three,
    grad_send_two,
    grad_recv_two,
    grad_send_three,
    grad_recv_three,
    cot_halves,
    att_halves,
    cot_all,
    att_all,
    part,
    block_rows,
    z_send,
    z_recv,
    y_send,
    y_recv,
    scores_one,
    scores_two,
    scores_three,
    level_out,
    level_lse,
    lse_wide,
    delta_wide,
    totals,
    send_sems,
    recv_sems,
    in_sems,
    out_sems,
):
    rank = lax.axis_index("seq")
    x, z, y = rank // 32, (rank % 32) // 4, rank % 4
    x_high, x_low = x // 2, x % 2
    plane, mine_three = rank - rank % 32, rank % 32
    block, mine_two = rank - rank % 8, rank % 8
    has_head = (y == 1) | (y == 2)
    own_head = 2 * z + jnp.where(y == 2, 1, 0)

    def worker(head):
        return 4 * (head // 2) + 1 + head % 2

    def outward(step, count):
        return count // 2 + (1 - 2 * (step % 2)) * ((step + 1) // 2)

    barrier = pltpu.get_barrier_semaphore()

    def greet(device):
        pl.semaphore_signal(barrier, inc=1, device_id={"seq": device}, device_id_type=MESH)

    @pl.loop(0, 31)
    def _(step):
        greet(plane + (mine_three + outward(step, 32)) % 32)

    @pl.loop(1, 4)
    def _(step):
        greet(((x + step) % 4) * 32 + mine_three)

    other_x = 2 * x_high + 1 - x_low

    @pl.loop(1, 4)
    def _(step):
        greet(other_x * 32 + z * 4 + (y + step) % 4)

    pairs = (
        (shift_far, shift_ref),
        (q_far, q_ref),
        (k_far, k_ref),
        (v_far, v_ref),
        (cot_far, cot_ref),
        (weight_far, weight_ref),
        (length_far, length_ref),
    )
    incoming = [pltpu.make_async_copy(*pair, in_sems.at[index]) for index, pair in enumerate(pairs)]
    for copy in incoming:
        copy.start()
    pairs = (
        (mixed_ref, mixed_far),
        (dq_ref, dq_far),
        (dk_ref, dk_far),
        (dv_ref, dv_far),
        (dw_ref, dw_far),
    )
    outgoing = [pltpu.make_async_copy(*pair, out_sems.at[index]) for index, pair in enumerate(pairs)]

    def push(from_ref, to_ref, index, device):
        pltpu.make_async_remote_copy(
            src_ref=from_ref,
            dst_ref=to_ref,
            send_sem=send_sems.at[index],
            recv_sem=recv_sems.at[index],
            device_id={"seq": device},
            device_id_type=MESH,
        ).start()

    def keep(from_ref, to_ref, index):
        pltpu.make_async_copy(from_ref, to_ref, recv_sems.at[index]).start()

    def arrived(ref, index):
        pltpu.make_async_copy(ref, ref, recv_sems.at[index]).wait()

    def left(ref, index):
        pltpu.make_async_copy(ref, ref, send_sems.at[index]).wait()

    for index in range(4):
        incoming[index].wait()
    for index, ref in enumerate((q_ref, k_ref, v_ref)):
        for tile in range(TILES):
            source[index, tile] = ref[:, 128 * tile : 128 * tile + 128].astype(F32)

    def column_shift(level, tile):
        shape = (COUNT[level], 128)
        heads = over_48(iota(shape, 1) + 128 * tile)
        value = jnp.zeros(shape, jnp.int32)
        for head in range(HEADS):
            if tile in tile_span(head * DIM, DIM):
                value = jnp.where(heads == head, shift_ref[level, head], value)
        return value

    shifts = [[column_shift(level, tile) for tile in range(TILES)] for level in range(2)]

    def pick(view, level):
        tiles = []
        for tile in range(TILES):
            value = view[tile, pl.ds(0, COUNT[level], RATE[level]), :]
            for offset in range(1, RATE[level]):
                rows = view[tile, pl.ds(offset, COUNT[level], RATE[level]), :]
                value = jnp.where(shifts[level][tile] == offset, rows, value)
            tiles.append(value)
        return tiles

    def spread(view, level, tiles, add):
        for tile in range(TILES):
            for offset in range(RATE[level]):
                place = (tile, pl.ds(offset, COUNT[level], RATE[level]), slice(None))
                other = view[place] if add else HIDDEN
                value = tiles[tile] + other if add else tiles[tile]
                view[place] = jnp.where(shifts[level][tile] == offset, value, other)

    picked_three = [pick(source.at[index], 1) for index in range(3)]
    for head in range(HEADS):
        low = iota((8, 128), 1) < 64
        near = take_window(picked_three[0], head * DIM, DIM, 0)
        far = take_window(picked_three[1], head * DIM, DIM, 64)
        totals[0, 0, 0:8] = jnp.where(low, near, far)
        totals[0, 0, 8:16] = take_window(picked_three[2], head * DIM, DIM, 0)
        send_three[head] = totals[0, 0, 0:16].astype(BF16)

    pl.semaphore_wait(barrier, 37)

    @pl.loop(0, HEADS)
    def _(step):
        head = (2 * z + outward(step, HEADS) + HEADS) % HEADS
        other = worker(head)

        @pl.when(other != mine_three)
        def _():
            push(send_three.at[head], recv_three.at[mine_three], 1, plane + other)

    @pl.when(has_head)
    def _():
        keep(send_three.at[own_head], recv_three.at[mine_three], 1)

    for index in range(3):
        picked = pick(source.at[index], 0)
        for other in range(8):
            send_two[other, index] = take_window(picked, 96 * other, 96, 0).astype(BF16)

    @pl.loop(1, 8)
    def _(step):
        other = (mine_two + step) % 8
        push(send_two.at[other], recv_two.at[:, pl.ds(32 * mine_two, 32)], 0, block + other)

    keep(send_two.at[mine_two], recv_two.at[:, pl.ds(32 * mine_two, 32)], 0)

    for index in range(4, 7):
        incoming[index].wait()
    cot_halves[0] = cot_ref[:, :HALF]
    cot_halves[1] = cot_ref[:, HALF:]

    @pl.loop(1, 4)
    def _(step):
        other = (x + step) % 4
        push(cot_halves.at[other // 2], cot_all.at[x], 2, other * 32 + mine_three)

    keep(cot_halves.at[x_high], cot_all.at[x], 2)
    ends = []
    running = 0
    for index in range(8):
        running = running + length_ref[index]
        ends.append(running)

    def slide(positions):
        value = jnp.zeros(positions.shape, jnp.int32)
        for end in ends:
            value = value + jnp.where(positions >= end, 1, 0)
        return value

    def seen(count, first, stride):
        rows = slide(first + stride * iota((count, 128), 0))
        columns = slide(first + stride * iota((8, count), 1))[0:1]
        rows = jnp.concatenate([rows] * (count // 128), axis=1)
        return rows == jnp.broadcast_to(columns, (count, count))

    def lane_mask(shape, first, width):
        lanes = iota(shape, 1)
        return (lanes >= first) & (lanes < first + width)

    def masked(value, first, width):
        inside = lane_mask(value.shape, first, width)
        return jnp.where(inside, value.astype(F32), 0.0).astype(BF16)

    def window(head):
        span = tile_span(head * DIM, DIM)
        return slice(128 * span[0], 128 * (span[-1] + 1)), head * DIM - 128 * span[0], span

    visible_one = seen(ROWS, ROWS * rank, 1)
    outs, tops, sums = ([None] * TILES for _ in range(3))

    def merge(tiles, head, value, wide):
        _, first, span = window(head)
        for index, tile in enumerate(span):
            piece = value[:, 128 * index : 128 * index + 128] if wide else value
            piece = jnp.broadcast_to(piece, (ROWS, 128))
            if tiles[tile] is None:
                tiles[tile] = piece
            else:
                columns = iota((ROWS, 128), 1) + 128 * index
                inside = (columns >= first) & (columns < first + DIM)
                tiles[tile] = jnp.where(inside, piece, tiles[tile])

    for head in range(HEADS):
        lanes, first, span = window(head)
        scores = matmul(masked(q_ref[:, lanes], first, DIM), k_ref[:, lanes], (1, 1)) * SCALE
        scores = jnp.where(visible_one, scores, HIDDEN)
        scores_one[head] = scores
        top = jnp.max(scores, axis=1, keepdims=True)
        weights = jnp.exp(scores - top)
        total = jnp.sum(weights, axis=1, keepdims=True)
        out = matmul(weights.astype(BF16), v_ref[:, lanes], (1, 0))
        merge(outs, head, out, True)
        merge(tops, head, top, False)
        merge(sums, head, total, False)
    for tile in range(TILES):
        level_out[0, tile] = outs[tile] / sums[tile]
        level_lse[0, tile] = tops[tile] + jnp.log(sums[tile])

    def split_three():
        both = recv_three[...].astype(F32).reshape(32, 2, 8, 128)
        first = both[:, 0].reshape(256, 128)
        return first, pltpu.roll(first, 64, 1), both[:, 1].reshape(256, 128).astype(BF16)

    def part_of(value, first):
        return jnp.where(lane_mask(value.shape, first, DIM), value, 0.0).astype(BF16)

    @pl.when(has_head)
    def _():
        arrived(recv_three, 1)
        first, turned, value_rows = split_three()
        scores = matmul(part_of(first, 0), turned.astype(BF16), (1, 1)) * SCALE
        visible = seen(256, 4096 * x + shift_ref[1, own_head], RATE[1])
        scores = jnp.where(visible, scores, HIDDEN)
        scores_three[...] = scores
        top = jnp.max(scores, axis=1, keepdims=True)
        weights = jnp.exp(scores - top)
        total = jnp.sum(weights, axis=1, keepdims=True)
        out = matmul(weights.astype(BF16), value_rows, (1, 0)) / total
        lse = jnp.broadcast_to(top + jnp.log(total), (256, 128))
        out = jnp.where(iota((256, 128), 1) < 64, out, lse)
        out_send_three[...] = out.reshape(32, 8, 128)

        @pl.loop(0, 31)
        def _(step):
            other = (mine_three + outward(step, 32)) % 32
            push(out_send_three.at[other], out_recv_three.at[own_head], 3, plane + other)

        keep(out_send_three.at[mine_three], out_recv_three.at[own_head], 3)

    arrived(recv_two, 0)
    out_two, lse_two = None, None
    lanes_two = iota((256, 128), 1)
    for member in range(2):
        head = 2 * mine_two + member
        scores = matmul(masked(recv_two[0], DIM * member, DIM), recv_two[1], (1, 1)) * SCALE
        visible = seen(256, ROWS * block + shift_ref[0, head], RATE[0])
        scores = jnp.where(visible, scores, HIDDEN)
        scores_two[member] = scores
        top = jnp.max(scores, axis=1, keepdims=True)
        weights = jnp.exp(scores - top)
        total = jnp.sum(weights, axis=1, keepdims=True)
        out = matmul(weights.astype(BF16), recv_two[2], (1, 0)) / total
        lse = jnp.broadcast_to(top + jnp.log(total), (256, 128))
        out_two = out if member == 0 else jnp.where(lanes_two < DIM, out_two, out)
        lse_two = lse if member == 0 else jnp.where(lanes_two < 112, lse_two, lse)
    high, middle, low = three_parts(lse_two)
    turn = lanes_two % 16
    lse_two = jnp.where(turn == 0, high, jnp.where(turn == 1, middle, jnp.where(turn == 2, low, 0.0)))
    out_send_two[...] = jnp.where(lanes_two < 96, out_two, lse_two).astype(BF16)

    @pl.loop(1, 8)
    def _(step):
        other = (mine_two + step) % 8
        push(out_send_two.at[pl.ds(32 * other, 32)], out_recv_two.at[mine_two], 4, block + other)

    keep(out_send_two.at[pl.ds(32 * mine_two, 32)], out_recv_two.at[mine_two], 4)

    d_attended = jnp.dot(cot_ref[...], weight_ref[...], preferred_element_type=F32).astype(BF16)
    for tile in range(TILES):
        source[3, tile] = d_attended[:, 128 * tile : 128 * tile + 128].astype(F32)
    picked = pick(source.at[3], 0)
    for other in range(8):
        d_send_two[other] = take_window(picked, 96 * other, 96, 0).astype(BF16)

    @pl.loop(1, 8)
    def _(step):
        other = (mine_two + step) % 8
        push(d_send_two.at[other], d_recv_two.at[pl.ds(32 * mine_two, 32)], 12, block + other)

    keep(d_send_two.at[mine_two], d_recv_two.at[pl.ds(32 * mine_two, 32)], 12)

    arrived(out_recv_three, 3)
    out_three = put_windows([out_recv_three[head] for head in range(HEADS)], DIM, 0)
    lse_three = put_windows([out_recv_three[head] for head in range(HEADS)], DIM, 64)
    spread(level_out.at[2], 1, out_three, False)
    spread(level_lse.at[2], 1, lse_three, False)
    arrived(out_recv_two, 4)
    row, column = iota((128, 128), 0), iota((128, 128), 1)
    widen = ((row >= 96) & (row < 99) & (column < DIM)) | (
        (row >= 112) & (row < 115) & (column >= DIM) & (column < 96)
    )
    widen = jnp.where(widen, 1.0, 0.0).astype(BF16)
    all_two = out_recv_two[...].reshape(256, 128)
    lse_all = matmul(all_two, widen, (1, 0)).reshape(8, 32, 128)
    out_all = all_two.astype(F32).reshape(8, 32, 128)
    spread(level_out.at[1], 0, put_windows([out_all[i] for i in range(8)], 96, 0), False)
    spread(level_lse.at[1], 0, put_windows([lse_all[i] for i in range(8)], 96, 0), False)
    for tile in range(TILES):
        levels = [level_lse[level, tile] for level in range(3)]
        best = jnp.maximum(jnp.maximum(levels[0], levels[1]), levels[2])
        mass = sum(jnp.exp(level - best) for level in levels)
        lse = best + jnp.log(mass)
        lse_wide[tile] = lse
        combined = jnp.zeros((ROWS, 128), F32)
        for level in range(3):
            share = jnp.exp(levels[level] - lse)
            combined = combined + jnp.where(share > 0, share * level_out[level, tile], 0.0)
        att_halves[tile // 3, tile % 3] = combined.astype(BF16)

    for chunk in range(3):

        for step in (2, 1, 3):
            other = (x + step) % 4
            device = other * 32 + mine_three
            push(att_halves.at[other % 2, chunk], att_all.at[chunk, x], 13 + chunk, device)

        keep(att_halves.at[x_low, chunk], att_all.at[chunk, x], 13 + chunk)

    same_head = over_48(iota((HALF, HALF), 0)) == over_48(iota((HALF, HALF), 1))
    same_head = jnp.where(same_head, 1.0, 0.0).astype(BF16)
    for half in range(2):
        product = jnp.concatenate([source[3, 3 * half + tile] for tile in range(3)], axis=1)
        product = product * jnp.concatenate([att_halves[half, tile].astype(F32) for tile in range(3)], axis=1)
        high, middle, low = three_parts(product)
        summed = matmul(high.astype(BF16), same_head, (1, 0))
        summed = summed + matmul(middle.astype(BF16), same_head, (1, 0))
        for tile in range(3):
            delta_wide[3 * half + tile] = summed[:, 128 * tile : 128 * tile + 128]

    picked_lse, picked_delta = pick(lse_wide, 1), pick(delta_wide, 1)
    picked_grad = pick(source.at[3], 1)
    lanes = iota((8, 128), 1)
    for head in range(HEADS):
        near = take_window(picked_lse, head * DIM, DIM, 0)
        middle = take_window(picked_delta, head * DIM, DIM, 32)
        far = take_window(picked_grad, head * DIM, DIM, 64)
        stat_send_three[head] = jnp.where(lanes < 32, near, jnp.where(lanes < 64, middle, far))
    picked_lse, picked_delta = pick(lse_wide, 0), pick(delta_wide, 0)
    coded = []
    for tile in range(TILES):
        columns = iota((32, 128), 1) + 128 * tile
        turn = (columns - DIM * over_48(columns)) >> 3
        value = jnp.zeros((32, 128), F32)
        pieces = three_parts(picked_lse[tile]) + three_parts(picked_delta[tile])
        for index, piece in enumerate(pieces):
            value = jnp.where(turn == index, piece, value)
        coded.append(value)
    for other in range(8):
        stat_send_two[other] = take_window(coded, 96 * other, 96, 0).astype(BF16)

    @pl.loop(1, 8)
    def _(step):
        other = (mine_two + step) % 8
        push(stat_send_two.at[other], stat_recv_two.at[pl.ds(32 * mine_two, 32)], 6, block + other)

    keep(stat_send_two.at[mine_two], stat_recv_two.at[pl.ds(32 * mine_two, 32)], 6)

    @pl.loop(0, HEADS)
    def _(step):
        head = (2 * z + outward(step, HEADS) + HEADS) % HEADS
        other = worker(head)

        @pl.when(other != mine_three)
        def _():
            push(stat_send_three.at[head], stat_recv_three.at[mine_three], 7, plane + other)

    @pl.when(has_head)
    def _():
        keep(stat_send_three.at[own_head], stat_recv_three.at[mine_three], 7)

    attended = jnp.concatenate([att_halves[tile // 3, tile % 3] for tile in range(TILES)], axis=1)
    mixed_ref[...] = matmul(attended, weight_ref[...], (1, 1)).astype(BF16)
    outgoing[0].start()

    sums_q, sums_k, sums_v = ([None] * TILES for _ in range(3))
    def one_back(head):
        lanes, first, span = window(head)
        place = slice(first, first + 1) if first < 128 else slice(first - 128, first - 127)
        lse = lse_wide[span[0]][:, place]
        delta = delta_wide[span[0]][:, place]
        grad = jnp.concatenate([source[3, tile] for tile in span], axis=1)
        grad_low = grad.astype(BF16)
        grad_head = part_of(grad, first)
        prob = jnp.exp(scores_one[head] - lse)
        dprob = matmul(grad_head, v_ref[:, lanes], (1, 1))
        dscore = (prob * (dprob - delta) * SCALE).astype(BF16)
        merge(sums_q, head, matmul(dscore, k_ref[:, lanes], (1, 0)), True)
        merge(sums_k, head, matmul(dscore, q_ref[:, lanes], (0, 0)), True)
        merge(sums_v, head, matmul(prob.astype(BF16), grad_low, (0, 0)), True)

    arrived(cot_all, 2)
    for chunk in range(3):
        for head in range(EARLY[chunk], EARLY[chunk + 1]):
            one_back(head)
        arrived(att_all.at[chunk], 13 + chunk)
        part[chunk] = matmul(
            cot_all[...].reshape(4 * ROWS, HALF), att_all[chunk].reshape(4 * ROWS, 128), (0, 0)
        )
        for other in range(8):
            near = part[chunk, 24 * other : 24 * other + 24]
            far = part[chunk, 192 + 24 * other : 216 + 24 * other]
            z_send[chunk, other] = jnp.concatenate([near, far], axis=0).astype(BF16)

        for step in (4, 3, 5, 2, 6, 1, 7):
            other = (z + step) % 8
            device = plane + 4 * other + y
            push(z_send.at[chunk, other], z_recv.at[chunk, z], 16 + chunk, device)

        keep(z_send.at[chunk, z], z_recv.at[chunk, z], 16 + chunk)

    @pl.when(has_head)
    def _():
        arrived(stat_recv_three, 7)
        first, turned, value_rows = split_three()
        stats = stat_recv_three[...].reshape(256, 128)
        grad_rows = part_of(pltpu.roll(stats, 64, 1), 0)
        prob = jnp.exp(scores_three[...] - stats[:, 0:1])
        dprob = matmul(grad_rows, value_rows, (1, 1))
        dscore = (prob * (dprob - stats[:, 32:33]) * SCALE).astype(BF16)
        grad_qk = matmul(dscore, part_of(turned, 0), (1, 0))
        grad_qk = grad_qk + matmul(dscore, part_of(turned, 64), (0, 0))
        grad_v = matmul(prob.astype(BF16), grad_rows, (0, 0))
        grads = jnp.concatenate([grad_qk.reshape(32, 8, 128), grad_v.reshape(32, 8, 128)], axis=1)
        grad_send_three[...] = grads.astype(BF16)

        @pl.loop(0, 31)
        def _(step):
            other = (mine_three + outward(step, 32)) % 32
            push(grad_send_three.at[other], grad_recv_three.at[own_head], 8, plane + other)

        keep(grad_send_three.at[mine_three], grad_recv_three.at[own_head], 8)

    arrived(d_recv_two, 12)
    arrived(stat_recv_two, 6)
    row = iota((128, 256), 0)
    stats = stat_recv_two[...]
    grads = [None] * 3
    for member in range(2):

        def gathered(first):
            hit = (row == first) | (row == first + 8) | (row == first + 16)
            return matmul(stats, jnp.where(hit, 1.0, 0.0).astype(BF16), (1, 0))

        prob = jnp.exp(scores_two[member] - gathered(DIM * member))
        dprob = matmul(masked(d_recv_two[...], DIM * member, DIM), recv_two[2], (1, 1))
        dscore = (prob * (dprob - gathered(DIM * member + 24)) * SCALE).astype(BF16)
        news = (
            matmul(dscore, recv_two[1], (1, 0)),
            matmul(dscore, recv_two[0], (0, 0)),
            matmul(prob.astype(BF16), d_recv_two[...], (0, 0)),
        )
        for index, new in enumerate(news):
            old = grads[index]
            grads[index] = new if member == 0 else jnp.where(lanes_two < DIM, old, new)
    for index in range(3):
        grad_send_two[index] = grads[index].astype(BF16)

    @pl.loop(1, 8)
    def _(step):
        other = (mine_two + step) % 8
        push(grad_send_two.at[:, pl.ds(32 * other, 32)], grad_recv_two.at[mine_two], 9, block + other)

    keep(grad_send_two.at[:, pl.ds(32 * mine_two, 32)], grad_recv_two.at[mine_two], 9)

    for chunk in range(3):
        arrived(z_recv.at[chunk], 16 + chunk)
        rows = z_recv[chunk, 0].astype(F32)
        for other in range(1, 8):
            rows = rows + z_recv[chunk, other].astype(F32)
        block_rows[:, 128 * chunk : 128 * chunk + 128] = rows
    for low in range(2):
        for other in range(4):
            start = 24 * low + 6 * other
            y_send[low, other, 0:6] = block_rows[start : start + 6]
            y_send[low, other, 6:8] = jnp.zeros((2, HALF), F32)

    @pl.loop(1, 8)
    def _(step):
        other = (4 * x_low + y + step) % 8
        low, high = other // 4, other % 4
        device = (2 * x_high + low) * 32 + 4 * z + high
        push(y_send.at[low, high], y_recv.at[x_low, y], 11, device)

    keep(y_send.at[x_low, y], y_recv.at[x_low, y], 11)

    for head in range(EARLY[3], HEADS):
        one_back(head)
    for tile in range(TILES):
        totals[0, tile] = sums_q[tile]
        totals[1, tile] = sums_k[tile]
        totals[2, tile] = sums_v[tile]

    arrived(grad_recv_three, 8)
    received = grad_recv_three[...].astype(F32)
    for index, (place, rows) in enumerate(((0, slice(0, 8)), (64, slice(0, 8)), (0, slice(8, 16)))):
        tiles = put_windows([received[head, rows] for head in range(HEADS)], DIM, place)
        spread(totals.at[index], 1, tiles, True)
    arrived(grad_recv_two, 9)
    for index, out_ref in enumerate((dq_ref, dk_ref, dv_ref)):
        windows = [grad_recv_two[other, index].astype(F32) for other in range(8)]
        spread(totals.at[index], 0, put_windows(windows, 96, 0), True)
        for tile in range(TILES):
            out_ref[:, 128 * tile : 128 * tile + 128] = totals[index, tile].astype(BF16)
        outgoing[1 + index].start()

    arrived(y_recv, 11)
    for low in range(2):
        rows = (y_recv[low, 0] + y_recv[low, 1]) + (y_recv[low, 2] + y_recv[low, 3])
        dw_ref[:, HALF * low : HALF * low + HALF] = rows[0:6] * (16384**-0.5)
    outgoing[4].start()

    left(send_two.at[0:7], 0)
    left(cot_all.at[0:3], 2)
    left(out_send_two.at[0:224], 4)
    for chunk in range(3):
        left(att_all.at[chunk, 0:3], 13 + chunk)
        left(z_send.at[chunk, 0:7], 16 + chunk)
    left(stat_send_two.at[0:7], 6)
    left(grad_recv_two.at[0:7], 9)
    left(d_send_two.at[0:7], 12)
    left(y_send.at[0:1], 11)
    left(y_send.at[0, 0:3], 11)

    @pl.when(has_head)
    def _():
        left(send_three.at[0:15], 1)
        left(stat_send_three.at[0:15], 7)
        left(out_send_three.at[0:31], 3)
        left(grad_send_three.at[0:31], 8)

    @pl.when(jnp.logical_not(has_head))
    def _():
        left(send_three, 1)
        left(stat_send_three, 7)

    for copy in outgoing:
        copy.wait()


def finish(*refs):
    sources, results, holders, sems = refs[:5], refs[5:10], refs[10:15], refs[15]
    inward, outward = [], []
    for index in range(5):
        inward.append(pltpu.make_async_copy(sources[index], holders[index], sems.at[0, index]))
        outward.append(pltpu.make_async_copy(holders[index], results[index], sems.at[1, index]))
        inward[index].start()
    for index in range(5):
        inward[index].wait()
        outward[index].start()
    for index in range(5):
        outward[index].wait()


def local(queries, keys, values, cotangent, out_weight, slide_lengths, head_dilation_shifts):
    far = pl.BlockSpec(memory_space=pltpu.HBM)
    wide = jax.ShapeDtypeStruct((ROWS, WIDTH), BF16)
    scratch = [
        ((4, TILES, ROWS, 128), F32),
        ((8, 3, 32, 128), BF16),
        ((3, 256, 128), BF16),
        ((8, 32, 128), BF16),
        ((256, 128), BF16),
        ((16, 16, 128), BF16),
        ((32, 16, 128), BF16),
        ((256, 128), BF16),
        ((8, 32, 128), BF16),
        ((32, 8, 128), F32),
        ((16, 8, 128), F32),
        ((8, 32, 128), BF16),
        ((256, 128), BF16),
        ((16, 8, 128), F32),
        ((32, 8, 128), F32),
        ((3, 256, 128), BF16),
        ((8, 3, 32, 128), BF16),
        ((32, 16, 128), BF16),
        ((16, 16, 128), BF16),
        ((2, ROWS, HALF), BF16),
        ((2, 3, ROWS, 128), BF16),
        ((4, ROWS, HALF), BF16),
        ((3, 4, ROWS, 128), BF16),
        ((3, HALF, 128), F32),
        ((48, HALF), F32),
        ((3, 8, 48, 128), BF16),
        ((3, 8, 48, 128), BF16),
        ((2, 4, 8, HALF), F32),
        ((2, 4, 8, HALF), F32),
        ((HEADS, ROWS, ROWS), F32),
        ((2, 256, 256), F32),
        ((256, 256), F32),
        ((3, TILES, ROWS, 128), F32),
        ((3, TILES, ROWS, 128), F32),
        ((TILES, ROWS, 128), F32),
        ((TILES, ROWS, 128), F32),
        ((3, TILES, ROWS, 128), F32),
    ]
    out_shape = (wide, wide, wide, wide, jax.ShapeDtypeStruct((WIDTH // 128, WIDTH), F32))
    results = pl.pallas_call(
        kernel,
        out_shape=out_shape,
        in_specs=[far] * 7,
        out_specs=(far,) * 5,
        scratch_shapes=[pltpu.VMEM((ROWS, WIDTH), BF16)] * 4
        + [pltpu.VMEM((WIDTH // 128, WIDTH), F32)]
        + [pltpu.VMEM((ROWS, WIDTH), BF16)] * 4
        + [pltpu.VMEM((WIDTH, WIDTH), BF16), pltpu.SMEM((8,), jnp.int32), pltpu.SMEM((2, HEADS), jnp.int32)]
        + [pltpu.VMEM(shape, dtype) for shape, dtype in scratch]
        + [pltpu.SemaphoreType.DMA((19,)), pltpu.SemaphoreType.DMA((19,)), pltpu.SemaphoreType.DMA((7,)), pltpu.SemaphoreType.DMA((5,))],
        compiler_params=pltpu.CompilerParams(
            collective_id=0, has_side_effects=True, vmem_limit_bytes=VMEM
        ),
        name="dilated_attention",
    )(queries, keys, values, cotangent, out_weight, slide_lengths, head_dilation_shifts)
    return pl.pallas_call(
        finish,
        out_shape=out_shape,
        in_specs=[far] * 5,
        out_specs=(far,) * 5,
        scratch_shapes=[pltpu.VMEM(shape.shape, shape.dtype) for shape in out_shape]
        + [pltpu.SemaphoreType.DMA((2, 5))],
        compiler_params=pltpu.CompilerParams(vmem_limit_bytes=VMEM),
        name="results_to_hbm",
    )(*results)


def solution(mesh):
    rows = P(("dp", "seq"), None)
    return jax.shard_map(
        local,
        mesh=mesh,
        in_specs=(rows, rows, rows, rows, P(), P("dp"), P()),
        out_specs=(rows,) * 5,
        check_vma=False,
    )
```

```python
import jax
import jax.numpy as jnp
from jax import lax
from jax.experimental import pallas as pl
from jax.experimental.pallas import tpu as pltpu
from jax.sharding import PartitionSpec as P

HEADS = 16
DIM = 48
WIDTH = HEADS * DIM
ROWS = 128
TILES = WIDTH // 128
HALF = WIDTH // 2
RATE = (4, 16)
COUNT = (ROWS // 4, ROWS // 16)
SCALE = DIM**-0.5
HIDDEN = -1e30
EARLY = (0, 3, 5, 7)
VMEM = 60 * 1024 * 1024
F32 = jnp.float32
BF16 = jnp.bfloat16
MESH = pl.DeviceIdType.MESH


def matmul(a, b, contract):
    return lax.dot_general(a, b, ((contract[:1], contract[1:]), ((), ())), preferred_element_type=F32)


def iota(shape, axis):
    return lax.broadcasted_iota(jnp.int32, shape, axis)


def over_48(columns):
    return (columns * 1366) >> 16


def tile_span(first, width):
    return range(first // 128, (first + width - 1) // 128 + 1)


def take_window(tiles, first, width, place):
    at, off = first // 128, first % 128
    turn = (place - off) % 128
    near = tiles[at] if turn == 0 else pltpu.roll(tiles[at], turn, 1)
    if off + width <= 128:
        return near
    far = tiles[at + 1] if turn == 0 else pltpu.roll(tiles[at + 1], turn, 1)
    return jnp.where(iota(near.shape, 1) < place + 128 - off, near, far)


def put_windows(windows, width, place):
    tiles = [None] * TILES
    for index, window in enumerate(windows):
        first = index * width
        off = first % 128
        turn = (off - place) % 128
        turned = window if turn == 0 else pltpu.roll(window, turn, 1)
        for tile in tile_span(first, width):
            if tiles[tile] is None:
                tiles[tile] = turned
            else:
                columns = iota(window.shape, 1) + 128 * tile
                inside = (columns >= first) & (columns < first + width)
                tiles[tile] = jnp.where(inside, turned, tiles[tile])
    return tiles


def three_parts(value):
    high = value.astype(BF16).astype(F32)
    rest = value - high
    middle = rest.astype(BF16).astype(F32)
    return high, middle, rest - middle


def kernel(
    q_far,
    k_far,
    v_far,
    cot_far,
    weight_far,
    length_far,
    shift_far,
    mixed_far,
    dq_far,
    dk_far,
    dv_far,
    dw_far,
    mixed_ref,
    dq_ref,
    dk_ref,
    dv_ref,
    dw_ref,
    q_ref,
    k_ref,
    v_ref,
    cot_ref,
    weight_ref,
    length_ref,
    shift_ref,
    source,
    send_two,
    recv_two,
    d_send_two,
    d_recv_two,
    send_three,
    recv_three,
    out_send_two,
    out_recv_two,
    out_send_three,
    out_recv_three,
    stat_send_two,
    stat_recv_two,
    stat_send_three,
    stat_recv_three,
    grad_send_two,
    grad_recv_two,
    grad_send_three,
    grad_recv_three,
    cot_halves,
    att_halves,
    cot_all,
    att_all,
    part,
    block_rows,
    z_send,
    z_recv,
    same_head_ref,
    widen_ref,
    last_rows,
    last_send,
    last_recv,
    w_send,
    w_recv,
    y_send,
    y_recv,
    scores_one,
    scores_two,
    scores_three,
    level_out,
    level_lse,
    lse_wide,
    delta_wide,
    totals,
    send_sems,
    recv_sems,
    in_sems,
    out_sems,
):
    rank = lax.axis_index("seq")
    x, z, y = rank // 32, (rank % 32) // 4, rank % 4
    x_high, x_low = x // 2, x % 2
    plane, mine_three = rank - rank % 32, rank % 32
    block, mine_two = rank - rank % 8, rank % 8
    has_head = (y == 1) | (y == 2)
    own_head = 2 * z + jnp.where(y == 2, 1, 0)

    def worker(head):
        return 4 * (head // 2) + 1 + head % 2

    def outward(step, count):
        return count // 2 + (1 - 2 * (step % 2)) * ((step + 1) // 2)

    barrier = pltpu.get_barrier_semaphore()

    def greet(device):
        pl.semaphore_signal(barrier, inc=1, device_id={"seq": device}, device_id_type=MESH)

    @pl.loop(0, 31)
    def _(step):
        greet(plane + (mine_three + outward(step, 32)) % 32)

    @pl.loop(1, 4)
    def _(step):
        greet(((x + step) % 4) * 32 + mine_three)

    other_x = 2 * x_high + 1 - x_low

    @pl.loop(1, 4)
    def _(step):
        greet(other_x * 32 + z * 4 + (y + step) % 4)

    @pl.loop(1, 8)
    def _(step):
        greet(other_x * 32 + (z + step) % 8 * 4 + y)

    pairs = (
        (shift_far, shift_ref),
        (q_far, q_ref),
        (k_far, k_ref),
        (v_far, v_ref),
        (cot_far, cot_ref),
        (weight_far, weight_ref),
        (length_far, length_ref),
    )
    incoming = [pltpu.make_async_copy(*pair, in_sems.at[index]) for index, pair in enumerate(pairs)]
    for copy in incoming:
        copy.start()
    pairs = (
        (mixed_ref, mixed_far),
        (dq_ref, dq_far),
        (dk_ref, dk_far),
        (dv_ref, dv_far),
        (dw_ref, dw_far),
    )
    outgoing = [pltpu.make_async_copy(*pair, out_sems.at[index]) for index, pair in enumerate(pairs)]

    def push(from_ref, to_ref, index, device):
        pltpu.make_async_remote_copy(
            src_ref=from_ref,
            dst_ref=to_ref,
            send_sem=send_sems.at[index],
            recv_sem=recv_sems.at[index],
            device_id={"seq": device},
            device_id_type=MESH,
        ).start()

    def keep(from_ref, to_ref, index):
        pltpu.make_async_copy(from_ref, to_ref, recv_sems.at[index]).start()

    def arrived(ref, index):
        pltpu.make_async_copy(ref, ref, recv_sems.at[index]).wait()

    def left(ref, index):
        pltpu.make_async_copy(ref, ref, send_sems.at[index]).wait()

    for index in range(4):
        incoming[index].wait()
    for index, ref in enumerate((q_ref, k_ref, v_ref)):
        for tile in range(TILES):
            source[index, tile] = ref[:, 128 * tile : 128 * tile + 128].astype(F32)

    def column_shift(level, tile):
        shape = (COUNT[level], 128)
        heads = over_48(iota(shape, 1) + 128 * tile)
        value = jnp.zeros(shape, jnp.int32)
        for head in range(HEADS):
            if tile in tile_span(head * DIM, DIM):
                value = jnp.where(heads == head, shift_ref[level, head], value)
        return value

    shifts = [[column_shift(level, tile) for tile in range(TILES)] for level in range(2)]

    def pick(view, level):
        tiles = []
        for tile in range(TILES):
            value = view[tile, pl.ds(0, COUNT[level], RATE[level]), :]
            for offset in range(1, RATE[level]):
                rows = view[tile, pl.ds(offset, COUNT[level], RATE[level]), :]
                value = jnp.where(shifts[level][tile] == offset, rows, value)
            tiles.append(value)
        return tiles

    def spread(view, level, tiles, add, fill=0.0):
        for tile in range(TILES):
            for offset in range(RATE[level]):
                place = (tile, pl.ds(offset, COUNT[level], RATE[level]), slice(None))
                other = view[place] if add else fill
                value = tiles[tile] + other if add else tiles[tile]
                view[place] = jnp.where(shifts[level][tile] == offset, value, other)

    picked_three = [pick(source.at[index], 1) for index in range(3)]
    for head in range(HEADS):
        low = iota((8, 128), 1) < 64
        near = take_window(picked_three[0], head * DIM, DIM, 0)
        far = take_window(picked_three[1], head * DIM, DIM, 64)
        totals[0, 0, 0:8] = jnp.where(low, near, far)
        totals[0, 0, 8:16] = take_window(picked_three[2], head * DIM, DIM, 0)
        send_three[head] = totals[0, 0, 0:16].astype(BF16)

    pl.semaphore_wait(barrier, 44)

    @pl.loop(0, HEADS)
    def _(step):
        head = (2 * z + outward(step, HEADS) + HEADS) % HEADS
        other = worker(head)

        @pl.when(other != mine_three)
        def _():
            push(send_three.at[head], recv_three.at[mine_three], 1, plane + other)

    @pl.when(has_head)
    def _():
        keep(send_three.at[own_head], recv_three.at[mine_three], 1)

    for index in range(3):
        picked = pick(source.at[index], 0)
        for other in range(8):
            send_two[other, index] = take_window(picked, 96 * other, 96, 0).astype(BF16)

    @pl.loop(1, 8)
    def _(step):
        other = (mine_two + step) % 8
        push(send_two.at[other], recv_two.at[:, pl.ds(32 * mine_two, 32)], 0, block + other)

    keep(send_two.at[mine_two], recv_two.at[:, pl.ds(32 * mine_two, 32)], 0)

    for index in range(4, 7):
        incoming[index].wait()
    cot_halves[0] = cot_ref[:, :HALF]
    cot_halves[1] = cot_ref[:, HALF:]

    @pl.loop(1, 4)
    def _(step):
        other = (x + step) % 4
        push(cot_halves.at[other // 2], cot_all.at[x], 2, other * 32 + mine_three)

    keep(cot_halves.at[x_high], cot_all.at[x], 2)
    ends = []
    running = 0
    for index in range(8):
        running = running + length_ref[index]
        ends.append(running)

    def slide(positions):
        value = jnp.zeros(positions.shape, jnp.int32)
        for end in ends:
            value = value + jnp.where(positions >= end, 1, 0)
        return value

    def seen(count, first, stride):
        rows = slide(first + stride * iota((count, 128), 0))
        columns = slide(first + stride * iota((8, count), 1))[0:1]
        rows = jnp.concatenate([rows] * (count // 128), axis=1)
        return rows == jnp.broadcast_to(columns, (count, count))

    def lane_mask(shape, first, width):
        lanes = iota(shape, 1)
        return (lanes >= first) & (lanes < first + width)

    def masked(value, first, width):
        inside = lane_mask(value.shape, first, width)
        return jnp.where(inside, value.astype(F32), 0.0).astype(BF16)

    def window(head):
        span = tile_span(head * DIM, DIM)
        return slice(128 * span[0], 128 * (span[-1] + 1)), head * DIM - 128 * span[0], span

    same_head = over_48(iota((HALF, HALF), 0)) == over_48(iota((HALF, HALF), 1))
    same_head_ref[...] = jnp.where(same_head, 1.0, 0.0).astype(BF16)
    row, column = iota((128, 128), 0), iota((128, 128), 1)
    widen = ((row >= 96) & (row < 99) & (column < DIM)) | (
        (row >= 112) & (row < 115) & (column >= DIM) & (column < 96)
    )
    widen_ref[...] = jnp.where(widen, 1.0, 0.0).astype(BF16)

    visible_one = seen(ROWS, ROWS * rank, 1)
    outs, tops, sums = ([None] * TILES for _ in range(3))

    def merge(tiles, head, value, wide):
        _, first, span = window(head)
        for index, tile in enumerate(span):
            piece = value[:, 128 * index : 128 * index + 128] if wide else value
            piece = jnp.broadcast_to(piece, (ROWS, 128))
            if tiles[tile] is None:
                tiles[tile] = piece
            else:
                columns = iota((ROWS, 128), 1) + 128 * index
                inside = (columns >= first) & (columns < first + DIM)
                tiles[tile] = jnp.where(inside, piece, tiles[tile])

    for head in range(HEADS):
        lanes, first, span = window(head)
        scores = matmul(masked(q_ref[:, lanes], first, DIM), k_ref[:, lanes], (1, 1)) * SCALE
        scores = jnp.where(visible_one, scores, HIDDEN)
        scores_one[head] = scores
        top = jnp.max(scores, axis=1, keepdims=True)
        weights = jnp.exp(scores - top)
        total = jnp.sum(weights, axis=1, keepdims=True)
        out = matmul(weights.astype(BF16), v_ref[:, lanes], (1, 0))
        merge(outs, head, out, True)
        merge(tops, head, top, False)
        merge(sums, head, total, False)
    for tile in range(TILES):
        level_out[0, tile] = outs[tile] / sums[tile]
        level_lse[0, tile] = tops[tile] + jnp.log(sums[tile])

    def split_three():
        both = recv_three[...].astype(F32).reshape(32, 2, 8, 128)
        first = both[:, 0].reshape(256, 128)
        return first, pltpu.roll(first, 64, 1), both[:, 1].reshape(256, 128).astype(BF16)

    def part_of(value, first):
        return jnp.where(lane_mask(value.shape, first, DIM), value, 0.0).astype(BF16)

    @pl.when(has_head)
    def _():
        arrived(recv_three, 1)
        first, turned, value_rows = split_three()
        scores = matmul(part_of(first, 0), turned.astype(BF16), (1, 1)) * SCALE
        visible = seen(256, 4096 * x + shift_ref[1, own_head], RATE[1])
        scores = jnp.where(visible, scores, HIDDEN)
        scores_three[...] = scores
        top = jnp.max(scores, axis=1, keepdims=True)
        weights = jnp.exp(scores - top)
        total = jnp.sum(weights, axis=1, keepdims=True)
        out = matmul(weights.astype(BF16), value_rows, (1, 0)) / total
        lse = jnp.broadcast_to(top + jnp.log(total), (256, 128))
        out = jnp.where(iota((256, 128), 1) < 64, out, lse)
        out_send_three[...] = out.reshape(32, 8, 128)

        @pl.loop(0, 31)
        def _(step):
            other = (mine_three + outward(step, 32)) % 32
            push(out_send_three.at[other], out_recv_three.at[own_head], 3, plane + other)

        keep(out_send_three.at[mine_three], out_recv_three.at[own_head], 3)

    arrived(recv_two, 0)
    out_two, lse_two = None, None
    lanes_two = iota((256, 128), 1)
    for member in range(2):
        head = 2 * mine_two + member
        scores = matmul(masked(recv_two[0], DIM * member, DIM), recv_two[1], (1, 1)) * SCALE
        visible = seen(256, ROWS * block + shift_ref[0, head], RATE[0])
        scores = jnp.where(visible, scores, HIDDEN)
        scores_two[member] = scores
        top = jnp.max(scores, axis=1, keepdims=True)
        weights = jnp.exp(scores - top)
        total = jnp.sum(weights, axis=1, keepdims=True)
        out = matmul(weights.astype(BF16), recv_two[2], (1, 0)) / total
        lse = jnp.broadcast_to(top + jnp.log(total), (256, 128))
        out_two = out if member == 0 else jnp.where(lanes_two < DIM, out_two, out)
        lse_two = lse if member == 0 else jnp.where(lanes_two < 112, lse_two, lse)
    high, middle, low = three_parts(lse_two)
    turn = lanes_two % 16
    lse_two = jnp.where(turn == 0, high, jnp.where(turn == 1, middle, jnp.where(turn == 2, low, 0.0)))
    out_send_two[...] = jnp.where(lanes_two < 96, out_two, lse_two).astype(BF16)

    @pl.loop(1, 8)
    def _(step):
        other = (mine_two + step) % 8
        push(out_send_two.at[pl.ds(32 * other, 32)], out_recv_two.at[mine_two], 4, block + other)

    keep(out_send_two.at[pl.ds(32 * mine_two, 32)], out_recv_two.at[mine_two], 4)

    d_attended = jnp.dot(cot_ref[...], weight_ref[...], preferred_element_type=F32).astype(BF16)
    for tile in range(TILES):
        source[3, tile] = d_attended[:, 128 * tile : 128 * tile + 128].astype(F32)
    picked = pick(source.at[3], 0)
    for other in range(8):
        d_send_two[other] = take_window(picked, 96 * other, 96, 0).astype(BF16)

    @pl.loop(1, 8)
    def _(step):
        other = (mine_two + step) % 8
        push(d_send_two.at[other], d_recv_two.at[pl.ds(32 * mine_two, 32)], 12, block + other)

    keep(d_send_two.at[mine_two], d_recv_two.at[pl.ds(32 * mine_two, 32)], 12)

    arrived(out_recv_three, 3)
    out_three = put_windows([out_recv_three[head] for head in range(HEADS)], DIM, 0)
    lse_three = put_windows([out_recv_three[head] for head in range(HEADS)], DIM, 64)
    spread(level_out.at[2], 1, out_three, False)
    spread(level_lse.at[2], 1, lse_three, False, HIDDEN)
    arrived(out_recv_two, 4)
    all_two = out_recv_two[...].reshape(256, 128)
    lse_all = matmul(all_two, widen_ref[...], (1, 0)).reshape(8, 32, 128)
    out_all = all_two.astype(F32).reshape(8, 32, 128)
    spread(level_out.at[1], 0, put_windows([out_all[i] for i in range(8)], 96, 0), False)
    spread(level_lse.at[1], 0, put_windows([lse_all[i] for i in range(8)], 96, 0), False, HIDDEN)
    for chunk in range(3):
        for half in range(2):
            tile = 3 * half + chunk
            levels = [level_lse[level, tile] for level in range(3)]
            best = jnp.maximum(jnp.maximum(levels[0], levels[1]), levels[2])
            shares = [jnp.exp(level - best) for level in levels]
            mass = shares[0] + shares[1] + shares[2]
            combined = shares[0] * level_out[0, tile]
            for level in range(1, 3):
                combined = combined + shares[level] * level_out[level, tile]
            att_halves[half, chunk] = (combined / mass).astype(BF16)
            lse_wide[tile] = best + jnp.log(mass)
        for step in (2, 1, 3):
            other = (x + step) % 4
            device = other * 32 + mine_three
            push(att_halves.at[other % 2, chunk], att_all.at[chunk, x], 13 + chunk, device)
        keep(att_halves.at[x_low, chunk], att_all.at[chunk, x], 13 + chunk)

    same_head = same_head_ref[...]
    for half in range(2):
        product = jnp.concatenate([source[3, 3 * half + tile] for tile in range(3)], axis=1)
        product = product * jnp.concatenate([att_halves[half, tile].astype(F32) for tile in range(3)], axis=1)
        high, middle, low = three_parts(product)
        summed = matmul(high.astype(BF16), same_head, (1, 0))
        summed = summed + matmul(middle.astype(BF16), same_head, (1, 0))
        for tile in range(3):
            delta_wide[3 * half + tile] = summed[:, 128 * tile : 128 * tile + 128]

    picked_lse, picked_delta = pick(lse_wide, 1), pick(delta_wide, 1)
    picked_grad = pick(source.at[3], 1)
    lanes = iota((8, 128), 1)
    for head in range(HEADS):
        near = take_window(picked_lse, head * DIM, DIM, 0)
        middle = take_window(picked_delta, head * DIM, DIM, 32)
        far = take_window(picked_grad, head * DIM, DIM, 64)
        stat_send_three[head] = jnp.where(lanes < 32, near, jnp.where(lanes < 64, middle, far))
    @pl.loop(0, HEADS)
    def _(step):
        head = (2 * z + outward(step, HEADS) + HEADS) % HEADS
        other = worker(head)

        @pl.when(other != mine_three)
        def _():
            push(stat_send_three.at[head], stat_recv_three.at[mine_three], 7, plane + other)

    @pl.when(has_head)
    def _():
        keep(stat_send_three.at[own_head], stat_recv_three.at[mine_three], 7)

    picked_lse, picked_delta = pick(lse_wide, 0), pick(delta_wide, 0)
    coded = []
    for tile in range(TILES):
        columns = iota((32, 128), 1) + 128 * tile
        turn = (columns - DIM * over_48(columns)) >> 3
        value = jnp.zeros((32, 128), F32)
        pieces = three_parts(picked_lse[tile]) + three_parts(picked_delta[tile])
        for index, piece in enumerate(pieces):
            value = jnp.where(turn == index, piece, value)
        coded.append(value)
    for other in range(8):
        stat_send_two[other] = take_window(coded, 96 * other, 96, 0).astype(BF16)

    @pl.loop(1, 8)
    def _(step):
        other = (mine_two + step) % 8
        push(stat_send_two.at[other], stat_recv_two.at[pl.ds(32 * mine_two, 32)], 6, block + other)

    keep(stat_send_two.at[mine_two], stat_recv_two.at[pl.ds(32 * mine_two, 32)], 6)

    sums_q, sums_k, sums_v = ([None] * TILES for _ in range(3))
    def one_back(head):
        lanes, first, span = window(head)
        place = slice(first, first + 1) if first < 128 else slice(first - 128, first - 127)
        lse = lse_wide[span[0]][:, place]
        delta = delta_wide[span[0]][:, place]
        grad = jnp.concatenate([source[3, tile] for tile in span], axis=1)
        grad_low = grad.astype(BF16)
        grad_head = part_of(grad, first)
        prob = jnp.exp(scores_one[head] - lse)
        dprob = matmul(grad_head, v_ref[:, lanes], (1, 1))
        dscore = (prob * (dprob - delta) * SCALE).astype(BF16)
        merge(sums_q, head, matmul(dscore, k_ref[:, lanes], (1, 0)), True)
        merge(sums_k, head, matmul(dscore, q_ref[:, lanes], (0, 0)), True)
        merge(sums_v, head, matmul(prob.astype(BF16), grad_low, (0, 0)), True)

    arrived(cot_all, 2)
    for chunk in range(3):
        for head in range(EARLY[chunk], EARLY[chunk + 1]):
            one_back(head)
        arrived(att_all.at[chunk], 13 + chunk)
        part[chunk] = matmul(
            cot_all[...].reshape(4 * ROWS, HALF), att_all[chunk].reshape(4 * ROWS, 128), (0, 0)
        )
        if chunk < 2:
            for other in range(8):
                near = part[chunk, 24 * other : 24 * other + 24]
                far = part[chunk, 192 + 24 * other : 216 + 24 * other]
                z_send[chunk, other] = jnp.concatenate([near, far], axis=0).astype(BF16)
            for step in (4, 3, 5, 2, 6, 1, 7):
                other = (z + step) % 8
                device = plane + 4 * other + y
                push(z_send.at[chunk, other], z_recv.at[chunk, z], 16 + chunk, device)
            keep(z_send.at[chunk, z], z_recv.at[chunk, z], 16 + chunk)

    for other in range(4):
        for group in range(16):
            start = 24 * group + 6 * other
            last_rows[8 * group : 8 * group + 6] = part[2, start : start + 6]
            last_rows[8 * group + 6 : 8 * group + 8] = jnp.zeros((2, 128), F32)
        last_send[other] = last_rows[...].astype(BF16)

    @pl.loop(1, 4)
    def _(step):
        other = (y + step) % 4
        push(last_send.at[other], last_recv.at[y], 18, plane + 4 * z + other)

    keep(last_send.at[y], last_recv.at[y], 18)

    @pl.when(has_head)
    def _():
        arrived(stat_recv_three, 7)
        first, turned, value_rows = split_three()
        stats = stat_recv_three[...].reshape(256, 128)
        grad_rows = part_of(pltpu.roll(stats, 64, 1), 0)
        prob = jnp.exp(scores_three[...] - stats[:, 0:1])
        dprob = matmul(grad_rows, value_rows, (1, 1))
        dscore = (prob * (dprob - stats[:, 32:33]) * SCALE).astype(BF16)
        grad_qk = matmul(dscore, part_of(turned, 0), (1, 0))
        grad_qk = grad_qk + matmul(dscore, part_of(turned, 64), (0, 0))
        grad_v = matmul(prob.astype(BF16), grad_rows, (0, 0))
        grads = jnp.concatenate([grad_qk.reshape(32, 8, 128), grad_v.reshape(32, 8, 128)], axis=1)
        grad_send_three[...] = grads.astype(BF16)

        @pl.loop(0, 31)
        def _(step):
            other = (mine_three + outward(step, 32)) % 32
            push(grad_send_three.at[other], grad_recv_three.at[own_head], 8, plane + other)

        keep(grad_send_three.at[mine_three], grad_recv_three.at[own_head], 8)

    arrived(d_recv_two, 12)
    arrived(stat_recv_two, 6)
    row = iota((128, 256), 0)
    stats = stat_recv_two[...]
    grads = [None] * 3
    for member in range(2):

        def gathered(first):
            hit = (row == first) | (row == first + 8) | (row == first + 16)
            return matmul(stats, jnp.where(hit, 1.0, 0.0).astype(BF16), (1, 0))

        prob = jnp.exp(scores_two[member] - gathered(DIM * member))
        dprob = matmul(masked(d_recv_two[...], DIM * member, DIM), recv_two[2], (1, 1))
        dscore = (prob * (dprob - gathered(DIM * member + 24)) * SCALE).astype(BF16)
        news = (
            matmul(dscore, recv_two[1], (1, 0)),
            matmul(dscore, recv_two[0], (0, 0)),
            matmul(prob.astype(BF16), d_recv_two[...], (0, 0)),
        )
        for index, new in enumerate(news):
            old = grads[index]
            grads[index] = new if member == 0 else jnp.where(lanes_two < DIM, old, new)
    for index in range(3):
        grad_send_two[index] = grads[index].astype(BF16)

    @pl.loop(1, 8)
    def _(step):
        other = (mine_two + step) % 8
        push(grad_send_two.at[:, pl.ds(32 * other, 32)], grad_recv_two.at[mine_two], 9, block + other)

    keep(grad_send_two.at[:, pl.ds(32 * mine_two, 32)], grad_recv_two.at[mine_two], 9)

    arrived(last_recv, 18)
    rows = (last_recv[0].astype(F32) + last_recv[1].astype(F32)) + (
        last_recv[2].astype(F32) + last_recv[3].astype(F32)
    )
    w_send[...] = rows.reshape(16, 8, 128)

    @pl.loop(0, 15)
    def _(step):
        other = (8 * x_low + z + outward(step, 16)) % 16
        low, high = other // 8, other % 8
        device = (2 * x_high + low) * 32 + 4 * high + y
        push(w_send.at[other], w_recv.at[8 * x_low + z], 10, device)

    keep(w_send.at[8 * x_low + z], w_recv.at[8 * x_low + z], 10)
    for chunk in range(2):
        arrived(z_recv.at[chunk], 16 + chunk)
        rows = z_recv[chunk, 0].astype(F32)
        for other in range(1, 8):
            rows = rows + z_recv[chunk, other].astype(F32)
        block_rows[:, 128 * chunk : 128 * chunk + 128] = rows
    for low in range(2):
        for other in range(4):
            start = 24 * low + 6 * other
            y_send[low, other, 0:6] = block_rows[start : start + 6]
            y_send[low, other, 6:8] = jnp.zeros((2, 256), F32)

    @pl.loop(1, 8)
    def _(step):
        other = (4 * x_low + y + step) % 8
        low, high = other // 4, other % 4
        device = (2 * x_high + low) * 32 + 4 * z + high
        push(y_send.at[low, high], y_recv.at[x_low, y], 11, device)

    keep(y_send.at[x_low, y], y_recv.at[x_low, y], 11)

    attended = jnp.concatenate([att_halves[tile // 3, tile % 3] for tile in range(TILES)], axis=1)
    mixed_ref[...] = matmul(attended, weight_ref[...], (1, 1)).astype(BF16)
    outgoing[0].start()
    for head in range(EARLY[3], HEADS):
        one_back(head)
    for tile in range(TILES):
        totals[0, tile] = sums_q[tile]
        totals[1, tile] = sums_k[tile]
        totals[2, tile] = sums_v[tile]

    arrived(grad_recv_three, 8)
    received = grad_recv_three[...].astype(F32)
    for index, (place, rows) in enumerate(((0, slice(0, 8)), (64, slice(0, 8)), (0, slice(8, 16)))):
        tiles = put_windows([received[head, rows] for head in range(HEADS)], DIM, place)
        spread(totals.at[index], 1, tiles, True)
    arrived(grad_recv_two, 9)
    for index, out_ref in enumerate((dq_ref, dk_ref, dv_ref)):
        windows = [grad_recv_two[other, index].astype(F32) for other in range(8)]
        spread(totals.at[index], 0, put_windows(windows, 96, 0), True)
        for tile in range(TILES):
            out_ref[:, 128 * tile : 128 * tile + 128] = totals[index, tile].astype(BF16)
        outgoing[1 + index].start()

    arrived(y_recv, 11)
    for low in range(2):
        rows = (y_recv[low, 0] + y_recv[low, 1]) + (y_recv[low, 2] + y_recv[low, 3])
        dw_ref[:, HALF * low : HALF * low + 256] = rows[0:6] * (16384**-0.5)
    arrived(w_recv, 10)
    for low in range(2):
        rows = w_recv[8 * low]
        for other in range(1, 8):
            rows = rows + w_recv[8 * low + other]
        dw_ref[:, HALF * low + 256 : HALF * low + HALF] = rows[0:6] * (16384**-0.5)
    outgoing[4].start()

    left(send_two.at[0:7], 0)
    left(cot_all.at[0:3], 2)
    left(out_send_two.at[0:224], 4)
    for chunk in range(3):
        left(att_all.at[chunk, 0:3], 13 + chunk)
    left(stat_send_two.at[0:7], 6)
    left(grad_recv_two.at[0:7], 9)
    left(d_send_two.at[0:7], 12)
    left(z_send.at[0, 0:7], 16)
    left(z_send.at[1, 0:7], 17)
    left(last_send.at[0:3], 18)
    left(w_send.at[0:15], 10)
    left(y_send.at[0:1], 11)
    left(y_send.at[0, 0:3], 11)

    @pl.when(has_head)
    def _():
        left(send_three.at[0:15], 1)
        left(stat_send_three.at[0:15], 7)
        left(out_send_three.at[0:31], 3)
        left(grad_send_three.at[0:31], 8)

    @pl.when(jnp.logical_not(has_head))
    def _():
        left(send_three, 1)
        left(stat_send_three, 7)

    for copy in outgoing:
        copy.wait()


def finish(*refs):
    sources, results, holders, sems = refs[:5], refs[5:10], refs[10:15], refs[15]
    inward, outward = [], []
    for index in range(5):
        inward.append(pltpu.make_async_copy(sources[index], holders[index], sems.at[0, index]))
        outward.append(pltpu.make_async_copy(holders[index], results[index], sems.at[1, index]))
        inward[index].start()
    for index in range(5):
        inward[index].wait()
        outward[index].start()
    for index in range(5):
        outward[index].wait()


def local(queries, keys, values, cotangent, out_weight, slide_lengths, head_dilation_shifts):
    far = pl.BlockSpec(memory_space=pltpu.HBM)
    wide = jax.ShapeDtypeStruct((ROWS, WIDTH), BF16)
    scratch = [
        ((4, TILES, ROWS, 128), F32),
        ((8, 3, 32, 128), BF16),
        ((3, 256, 128), BF16),
        ((8, 32, 128), BF16),
        ((256, 128), BF16),
        ((16, 16, 128), BF16),
        ((32, 16, 128), BF16),
        ((256, 128), BF16),
        ((8, 32, 128), BF16),
        ((32, 8, 128), F32),
        ((16, 8, 128), F32),
        ((8, 32, 128), BF16),
        ((256, 128), BF16),
        ((16, 8, 128), F32),
        ((32, 8, 128), F32),
        ((3, 256, 128), BF16),
        ((8, 3, 32, 128), BF16),
        ((32, 16, 128), BF16),
        ((16, 16, 128), BF16),
        ((2, ROWS, HALF), BF16),
        ((2, 3, ROWS, 128), BF16),
        ((4, ROWS, HALF), BF16),
        ((3, 4, ROWS, 128), BF16),
        ((3, HALF, 128), F32),
        ((48, 256), F32),
        ((2, 8, 48, 128), BF16),
        ((2, 8, 48, 128), BF16),
        ((HALF, HALF), BF16),
        ((128, 128), BF16),
        ((128, 128), F32),
        ((4, 128, 128), BF16),
        ((4, 128, 128), BF16),
        ((16, 8, 128), F32),
        ((16, 8, 128), F32),
        ((2, 4, 8, 256), F32),
        ((2, 4, 8, 256), F32),
        ((HEADS, ROWS, ROWS), F32),
        ((2, 256, 256), F32),
        ((256, 256), F32),
        ((3, TILES, ROWS, 128), F32),
        ((3, TILES, ROWS, 128), F32),
        ((TILES, ROWS, 128), F32),
        ((TILES, ROWS, 128), F32),
        ((3, TILES, ROWS, 128), F32),
    ]
    out_shape = (wide, wide, wide, wide, jax.ShapeDtypeStruct((WIDTH // 128, WIDTH), F32))
    results = pl.pallas_call(
        kernel,
        out_shape=out_shape,
        in_specs=[far] * 7,
        out_specs=(far,) * 5,
        scratch_shapes=[pltpu.VMEM((ROWS, WIDTH), BF16)] * 4
        + [pltpu.VMEM((WIDTH // 128, WIDTH), F32)]
        + [pltpu.VMEM((ROWS, WIDTH), BF16)] * 4
        + [pltpu.VMEM((WIDTH, WIDTH), BF16), pltpu.SMEM((8,), jnp.int32), pltpu.SMEM((2, HEADS), jnp.int32)]
        + [pltpu.VMEM(shape, dtype) for shape, dtype in scratch]
        + [pltpu.SemaphoreType.DMA((19,)), pltpu.SemaphoreType.DMA((19,)), pltpu.SemaphoreType.DMA((7,)), pltpu.SemaphoreType.DMA((5,))],
        compiler_params=pltpu.CompilerParams(
            collective_id=0, has_side_effects=True, vmem_limit_bytes=VMEM
        ),
        name="dilated_attention",
    )(queries, keys, values, cotangent, out_weight, slide_lengths, head_dilation_shifts)
    return pl.pallas_call(
        finish,
        out_shape=out_shape,
        in_specs=[far] * 5,
        out_specs=(far,) * 5,
        scratch_shapes=[pltpu.VMEM(shape.shape, shape.dtype) for shape in out_shape]
        + [pltpu.SemaphoreType.DMA((2, 5))],
        compiler_params=pltpu.CompilerParams(vmem_limit_bytes=VMEM),
        name="results_to_hbm",
    )(*results)


def solution(mesh):
    rows = P(("dp", "seq"), None)
    return jax.shard_map(
        local,
        mesh=mesh,
        in_specs=(rows, rows, rows, rows, P(), P("dp"), P()),
        out_specs=(rows,) * 5,
        check_vma=False,
    )
```

```python
import jax
import jax.numpy as jnp
from jax import lax
from jax.experimental import pallas as pl
from jax.experimental.pallas import tpu as pltpu
from jax.sharding import PartitionSpec as P

HEADS = 16
DIM = 48
WIDTH = HEADS * DIM
ROWS = 128
TILES = WIDTH // 128
HALF = WIDTH // 2
RATE = (4, 16)
COUNT = (ROWS // 4, ROWS // 16)
SCALE = DIM**-0.5
HIDDEN = -1e30
FIRST = 8
EARLY = (0, 3, 5, 7)
VMEM = 60 * 1024 * 1024
F32 = jnp.float32
BF16 = jnp.bfloat16
MESH = pl.DeviceIdType.MESH


def matmul(a, b, contract):
    return lax.dot_general(a, b, ((contract[:1], contract[1:]), ((), ())), preferred_element_type=F32)


def iota(shape, axis):
    return lax.broadcasted_iota(jnp.int32, shape, axis)


def over_48(columns):
    return (columns * 1366) >> 16


def tile_span(first, width):
    return range(first // 128, (first + width - 1) // 128 + 1)


def take_window(tiles, first, width, place):
    at, off = first // 128, first % 128
    turn = (place - off) % 128
    near = tiles[at] if turn == 0 else pltpu.roll(tiles[at], turn, 1)
    if off + width <= 128:
        return near
    far = tiles[at + 1] if turn == 0 else pltpu.roll(tiles[at + 1], turn, 1)
    return jnp.where(iota(near.shape, 1) < place + 128 - off, near, far)


def put_windows(windows, width, place):
    tiles = [None] * TILES
    for index, window in enumerate(windows):
        first = index * width
        off = first % 128
        turn = (off - place) % 128
        turned = window if turn == 0 else pltpu.roll(window, turn, 1)
        for tile in tile_span(first, width):
            if tiles[tile] is None:
                tiles[tile] = turned
            else:
                columns = iota(window.shape, 1) + 128 * tile
                inside = (columns >= first) & (columns < first + width)
                tiles[tile] = jnp.where(inside, turned, tiles[tile])
    return tiles


def three_parts(value):
    high = value.astype(BF16).astype(F32)
    rest = value - high
    middle = rest.astype(BF16).astype(F32)
    return high, middle, rest - middle


def kernel(
    q_far,
    k_far,
    v_far,
    cot_far,
    weight_far,
    length_far,
    shift_far,
    mixed_far,
    dq_far,
    dk_far,
    dv_far,
    dw_far,
    mixed_ref,
    dq_ref,
    dk_ref,
    dv_ref,
    dw_ref,
    q_ref,
    k_ref,
    v_ref,
    cot_ref,
    weight_ref,
    length_ref,
    shift_ref,
    source,
    send_two,
    recv_two,
    d_send_two,
    d_recv_two,
    send_three,
    recv_three,
    out_send_two,
    out_recv_two,
    out_send_three,
    out_recv_three,
    stat_send_two,
    stat_recv_two,
    stat_send_three,
    stat_recv_three,
    grad_send_two,
    grad_recv_two,
    grad_send_three,
    grad_recv_three,
    cot_halves,
    att_halves,
    cot_all,
    att_all,
    part,
    block_rows,
    z_send,
    z_recv,
    same_head_ref,
    widen_ref,
    last_rows,
    last_send,
    last_recv,
    w_send,
    w_recv,
    y_send,
    y_recv,
    scores_one,
    scores_two,
    scores_three,
    level_out,
    level_lse,
    lse_wide,
    delta_wide,
    totals,
    send_sems,
    recv_sems,
    in_sems,
    out_sems,
):
    rank = lax.axis_index("seq")
    x, z, y = rank // 32, (rank % 32) // 4, rank % 4
    x_high, x_low = x // 2, x % 2
    plane, mine_three = rank - rank % 32, rank % 32
    block, mine_two = rank - rank % 8, rank % 8
    has_head = (y == 1) | (y == 2)
    own_head = 2 * z + jnp.where(y == 2, 1, 0)

    def worker(head):
        return 4 * (head // 2) + 1 + head % 2

    def outward(step, count):
        return count // 2 + (1 - 2 * (step % 2)) * ((step + 1) // 2)

    barrier = pltpu.get_barrier_semaphore()

    def greet(device):
        pl.semaphore_signal(barrier, inc=1, device_id={"seq": device}, device_id_type=MESH)

    @pl.loop(0, 31)
    def _(step):
        greet(plane + (mine_three + outward(step, 32)) % 32)

    @pl.loop(1, 4)
    def _(step):
        greet(((x + step) % 4) * 32 + mine_three)

    other_x = 2 * x_high + 1 - x_low

    @pl.loop(1, 4)
    def _(step):
        greet(other_x * 32 + z * 4 + (y + step) % 4)

    @pl.loop(1, 8)
    def _(step):
        greet(other_x * 32 + (z + step) % 8 * 4 + y)

    pairs = (
        (shift_far, shift_ref),
        (q_far, q_ref),
        (k_far, k_ref),
        (v_far, v_ref),
        (cot_far, cot_ref),
        (weight_far, weight_ref),
        (length_far, length_ref),
    )
    incoming = [pltpu.make_async_copy(*pair, in_sems.at[index]) for index, pair in enumerate(pairs)]
    for copy in incoming:
        copy.start()
    pairs = (
        (mixed_ref, mixed_far),
        (dq_ref, dq_far),
        (dk_ref, dk_far),
        (dv_ref, dv_far),
        (dw_ref, dw_far),
    )
    outgoing = [pltpu.make_async_copy(*pair, out_sems.at[index]) for index, pair in enumerate(pairs)]

    def push(from_ref, to_ref, index, device):
        pltpu.make_async_remote_copy(
            src_ref=from_ref,
            dst_ref=to_ref,
            send_sem=send_sems.at[index],
            recv_sem=recv_sems.at[index],
            device_id={"seq": device},
            device_id_type=MESH,
        ).start()

    def keep(from_ref, to_ref, index):
        pltpu.make_async_copy(from_ref, to_ref, recv_sems.at[index]).start()

    def arrived(ref, index):
        pltpu.make_async_copy(ref, ref, recv_sems.at[index]).wait()

    def left(ref, index):
        pltpu.make_async_copy(ref, ref, send_sems.at[index]).wait()

    for index in range(4):
        incoming[index].wait()
    for index, ref in enumerate((q_ref, k_ref, v_ref)):
        for tile in range(TILES):
            source[index, tile] = ref[:, 128 * tile : 128 * tile + 128].astype(F32)

    def column_shift(level, tile):
        shape = (COUNT[level], 128)
        heads = over_48(iota(shape, 1) + 128 * tile)
        value = jnp.zeros(shape, jnp.int32)
        for head in range(HEADS):
            if tile in tile_span(head * DIM, DIM):
                value = jnp.where(heads == head, shift_ref[level, head], value)
        return value

    shifts = [[column_shift(level, tile) for tile in range(TILES)] for level in range(2)]

    def pick(view, level):
        tiles = []
        for tile in range(TILES):
            value = view[tile, pl.ds(0, COUNT[level], RATE[level]), :]
            for offset in range(1, RATE[level]):
                rows = view[tile, pl.ds(offset, COUNT[level], RATE[level]), :]
                value = jnp.where(shifts[level][tile] == offset, rows, value)
            tiles.append(value)
        return tiles

    def spread(view, level, tiles, add, fill=0.0):
        for tile in range(TILES):
            for offset in range(RATE[level]):
                place = (tile, pl.ds(offset, COUNT[level], RATE[level]), slice(None))
                other = view[place] if add else fill
                value = tiles[tile] + other if add else tiles[tile]
                view[place] = jnp.where(shifts[level][tile] == offset, value, other)

    picked_three = [pick(source.at[index], 1) for index in range(3)]
    for head in range(HEADS):
        low = iota((8, 128), 1) < 64
        near = take_window(picked_three[0], head * DIM, DIM, 0)
        far = take_window(picked_three[1], head * DIM, DIM, 64)
        totals[0, 0, 0:8] = jnp.where(low, near, far)
        totals[0, 0, 8:16] = take_window(picked_three[2], head * DIM, DIM, 0)
        send_three[head] = totals[0, 0, 0:16].astype(BF16)

    pl.semaphore_wait(barrier, 44)

    @pl.loop(0, HEADS)
    def _(step):
        head = (2 * z + outward(step, HEADS) + HEADS) % HEADS
        other = worker(head)

        @pl.when(other != mine_three)
        def _():
            push(send_three.at[head], recv_three.at[mine_three], 1, plane + other)

    @pl.when(has_head)
    def _():
        keep(send_three.at[own_head], recv_three.at[mine_three], 1)

    for index in range(3):
        picked = pick(source.at[index], 0)
        for other in range(8):
            send_two[other, index] = take_window(picked, 96 * other, 96, 0).astype(BF16)

    @pl.loop(1, 8)
    def _(step):
        other = (mine_two + step) % 8
        push(send_two.at[other], recv_two.at[:, pl.ds(32 * mine_two, 32)], 0, block + other)

    keep(send_two.at[mine_two], recv_two.at[:, pl.ds(32 * mine_two, 32)], 0)

    for index in range(4, 7):
        incoming[index].wait()
    cot_halves[0] = cot_ref[:, :HALF]
    cot_halves[1] = cot_ref[:, HALF:]

    @pl.loop(1, 4)
    def _(step):
        other = (x + step) % 4
        push(cot_halves.at[other // 2], cot_all.at[x], 2, other * 32 + mine_three)

    keep(cot_halves.at[x_high], cot_all.at[x], 2)
    ends = []
    running = 0
    for index in range(8):
        running = running + length_ref[index]
        ends.append(running)

    def slide(positions):
        value = jnp.zeros(positions.shape, jnp.int32)
        for end in ends:
            value = value + jnp.where(positions >= end, 1, 0)
        return value

    def seen(count, first, stride):
        rows = slide(first + stride * iota((count, 128), 0))
        columns = slide(first + stride * iota((8, count), 1))[0:1]
        rows = jnp.concatenate([rows] * (count // 128), axis=1)
        return rows == jnp.broadcast_to(columns, (count, count))

    def lane_mask(shape, first, width):
        lanes = iota(shape, 1)
        return (lanes >= first) & (lanes < first + width)

    def masked(value, first, width):
        inside = lane_mask(value.shape, first, width)
        return jnp.where(inside, value.astype(F32), 0.0).astype(BF16)

    def window(head):
        span = tile_span(head * DIM, DIM)
        return slice(128 * span[0], 128 * (span[-1] + 1)), head * DIM - 128 * span[0], span

    same_head = over_48(iota((HALF, HALF), 0)) == over_48(iota((HALF, HALF), 1))
    same_head_ref[...] = jnp.where(same_head, 1.0, 0.0).astype(BF16)
    row, column = iota((128, 128), 0), iota((128, 128), 1)
    widen = ((row >= 96) & (row < 99) & (column < DIM)) | (
        (row >= 112) & (row < 115) & (column >= DIM) & (column < 96)
    )
    widen_ref[...] = jnp.where(widen, 1.0, 0.0).astype(BF16)

    visible_one = seen(ROWS, ROWS * rank, 1)
    outs, tops, sums = ([None] * TILES for _ in range(3))

    def merge(tiles, head, value, wide):
        _, first, span = window(head)
        for index, tile in enumerate(span):
            piece = value[:, 128 * index : 128 * index + 128] if wide else value
            piece = jnp.broadcast_to(piece, (ROWS, 128))
            if tiles[tile] is None:
                tiles[tile] = piece
            else:
                columns = iota((ROWS, 128), 1) + 128 * index
                inside = (columns >= first) & (columns < first + DIM)
                tiles[tile] = jnp.where(inside, piece, tiles[tile])

    def one_forward(head):
        lanes, first, span = window(head)
        scores = matmul(masked(q_ref[:, lanes], first, DIM), k_ref[:, lanes], (1, 1)) * SCALE
        scores = jnp.where(visible_one, scores, HIDDEN)
        scores_one[head] = scores
        top = jnp.max(scores, axis=1, keepdims=True)
        weights = jnp.exp(scores - top)
        total = jnp.sum(weights, axis=1, keepdims=True)
        out = matmul(weights.astype(BF16), v_ref[:, lanes], (1, 0))
        merge(outs, head, out, True)
        merge(tops, head, top, False)
        merge(sums, head, total, False)

    for head in range(FIRST):
        one_forward(head)

    def split_three():
        both = recv_three[...].astype(F32).reshape(32, 2, 8, 128)
        first = both[:, 0].reshape(256, 128)
        return first, pltpu.roll(first, 64, 1), both[:, 1].reshape(256, 128).astype(BF16)

    def part_of(value, first):
        return jnp.where(lane_mask(value.shape, first, DIM), value, 0.0).astype(BF16)

    @pl.when(has_head)
    def _():
        arrived(recv_three, 1)
        first, turned, value_rows = split_three()
        scores = matmul(part_of(first, 0), turned.astype(BF16), (1, 1)) * SCALE
        visible = seen(256, 4096 * x + shift_ref[1, own_head], RATE[1])
        scores = jnp.where(visible, scores, HIDDEN)
        scores_three[...] = scores
        top = jnp.max(scores, axis=1, keepdims=True)
        weights = jnp.exp(scores - top)
        total = jnp.sum(weights, axis=1, keepdims=True)
        out = matmul(weights.astype(BF16), value_rows, (1, 0)) / total
        lse = jnp.broadcast_to(top + jnp.log(total), (256, 128))
        out = jnp.where(iota((256, 128), 1) < 64, out, lse)
        out_send_three[...] = out.reshape(32, 8, 128)

        @pl.loop(0, 31)
        def _(step):
            other = (mine_three + outward(step, 32)) % 32
            push(out_send_three.at[other], out_recv_three.at[own_head], 3, plane + other)

        keep(out_send_three.at[mine_three], out_recv_three.at[own_head], 3)

    arrived(recv_two, 0)
    out_two, lse_two = None, None
    lanes_two = iota((256, 128), 1)
    for member in range(2):
        head = 2 * mine_two + member
        scores = matmul(masked(recv_two[0], DIM * member, DIM), recv_two[1], (1, 1)) * SCALE
        visible = seen(256, ROWS * block + shift_ref[0, head], RATE[0])
        scores = jnp.where(visible, scores, HIDDEN)
        scores_two[member] = scores
        top = jnp.max(scores, axis=1, keepdims=True)
        weights = jnp.exp(scores - top)
        total = jnp.sum(weights, axis=1, keepdims=True)
        out = matmul(weights.astype(BF16), recv_two[2], (1, 0)) / total
        lse = jnp.broadcast_to(top + jnp.log(total), (256, 128))
        out_two = out if member == 0 else jnp.where(lanes_two < DIM, out_two, out)
        lse_two = lse if member == 0 else jnp.where(lanes_two < 112, lse_two, lse)
    high, middle, low = three_parts(lse_two)
    turn = lanes_two % 16
    lse_two = jnp.where(turn == 0, high, jnp.where(turn == 1, middle, jnp.where(turn == 2, low, 0.0)))
    out_send_two[...] = jnp.where(lanes_two < 96, out_two, lse_two).astype(BF16)

    @pl.loop(1, 8)
    def _(step):
        other = (mine_two + step) % 8
        push(out_send_two.at[pl.ds(32 * other, 32)], out_recv_two.at[mine_two], 4, block + other)

    keep(out_send_two.at[pl.ds(32 * mine_two, 32)], out_recv_two.at[mine_two], 4)

    d_attended = jnp.dot(cot_ref[...], weight_ref[...], preferred_element_type=F32).astype(BF16)
    for tile in range(TILES):
        source[3, tile] = d_attended[:, 128 * tile : 128 * tile + 128].astype(F32)
    picked = pick(source.at[3], 0)
    for other in range(8):
        d_send_two[other] = take_window(picked, 96 * other, 96, 0).astype(BF16)

    @pl.loop(1, 8)
    def _(step):
        other = (mine_two + step) % 8
        push(d_send_two.at[other], d_recv_two.at[pl.ds(32 * mine_two, 32)], 12, block + other)

    keep(d_send_two.at[mine_two], d_recv_two.at[pl.ds(32 * mine_two, 32)], 12)

    for head in range(FIRST, HEADS):
        one_forward(head)
    for tile in range(TILES):
        level_out[0, tile] = outs[tile] / sums[tile]
        level_lse[0, tile] = tops[tile] + jnp.log(sums[tile])

    arrived(out_recv_three, 3)
    out_three = put_windows([out_recv_three[head] for head in range(HEADS)], DIM, 0)
    lse_three = put_windows([out_recv_three[head] for head in range(HEADS)], DIM, 64)
    spread(level_out.at[2], 1, out_three, False)
    spread(level_lse.at[2], 1, lse_three, False, HIDDEN)
    arrived(out_recv_two, 4)
    all_two = out_recv_two[...].reshape(256, 128)
    lse_all = matmul(all_two, widen_ref[...], (1, 0)).reshape(8, 32, 128)
    out_all = all_two.astype(F32).reshape(8, 32, 128)
    spread(level_out.at[1], 0, put_windows([out_all[i] for i in range(8)], 96, 0), False)
    spread(level_lse.at[1], 0, put_windows([lse_all[i] for i in range(8)], 96, 0), False, HIDDEN)
    for chunk in range(3):
        for half in range(2):
            tile = 3 * half + chunk
            levels = [level_lse[level, tile] for level in range(3)]
            best = jnp.maximum(jnp.maximum(levels[0], levels[1]), levels[2])
            shares = [jnp.exp(level - best) for level in levels]
            mass = shares[0] + shares[1] + shares[2]
            combined = shares[0] * level_out[0, tile]
            for level in range(1, 3):
                combined = combined + shares[level] * level_out[level, tile]
            att_halves[half, chunk] = (combined / mass).astype(BF16)
            lse_wide[tile] = best + jnp.log(mass)
        for step in (2, 1, 3):
            other = (x + step) % 4
            device = other * 32 + mine_three
            push(att_halves.at[other % 2, chunk], att_all.at[chunk, x], 13 + chunk, device)
        keep(att_halves.at[x_low, chunk], att_all.at[chunk, x], 13 + chunk)

    same_head = same_head_ref[...]
    for half in range(2):
        product = jnp.concatenate([source[3, 3 * half + tile] for tile in range(3)], axis=1)
        product = product * jnp.concatenate([att_halves[half, tile].astype(F32) for tile in range(3)], axis=1)
        high, middle, low = three_parts(product)
        summed = matmul(high.astype(BF16), same_head, (1, 0))
        summed = summed + matmul(middle.astype(BF16), same_head, (1, 0))
        for tile in range(3):
            delta_wide[3 * half + tile] = summed[:, 128 * tile : 128 * tile + 128]

    picked_lse, picked_delta = pick(lse_wide, 1), pick(delta_wide, 1)
    picked_grad = pick(source.at[3], 1)
    lanes = iota((8, 128), 1)
    for head in range(HEADS):
        near = take_window(picked_lse, head * DIM, DIM, 0)
        middle = take_window(picked_delta, head * DIM, DIM, 32)
        far = take_window(picked_grad, head * DIM, DIM, 64)
        stat_send_three[head] = jnp.where(lanes < 32, near, jnp.where(lanes < 64, middle, far))
    @pl.loop(0, HEADS)
    def _(step):
        head = (2 * z + outward(step, HEADS) + HEADS) % HEADS
        other = worker(head)

        @pl.when(other != mine_three)
        def _():
            push(stat_send_three.at[head], stat_recv_three.at[mine_three], 7, plane + other)

    @pl.when(has_head)
    def _():
        keep(stat_send_three.at[own_head], stat_recv_three.at[mine_three], 7)

    picked_lse, picked_delta = pick(lse_wide, 0), pick(delta_wide, 0)
    coded = []
    for tile in range(TILES):
        columns = iota((32, 128), 1) + 128 * tile
        turn = (columns - DIM * over_48(columns)) >> 3
        value = jnp.zeros((32, 128), F32)
        pieces = three_parts(picked_lse[tile]) + three_parts(picked_delta[tile])
        for index, piece in enumerate(pieces):
            value = jnp.where(turn == index, piece, value)
        coded.append(value)
    for other in range(8):
        stat_send_two[other] = take_window(coded, 96 * other, 96, 0).astype(BF16)

    @pl.loop(1, 8)
    def _(step):
        other = (mine_two + step) % 8
        push(stat_send_two.at[other], stat_recv_two.at[pl.ds(32 * mine_two, 32)], 6, block + other)

    keep(stat_send_two.at[mine_two], stat_recv_two.at[pl.ds(32 * mine_two, 32)], 6)

    sums_q, sums_k, sums_v = ([None] * TILES for _ in range(3))
    def one_back(head):
        lanes, first, span = window(head)
        place = slice(first, first + 1) if first < 128 else slice(first - 128, first - 127)
        lse = lse_wide[span[0]][:, place]
        delta = delta_wide[span[0]][:, place]
        grad = jnp.concatenate([source[3, tile] for tile in span], axis=1)
        grad_low = grad.astype(BF16)
        grad_head = part_of(grad, first)
        prob = jnp.exp(scores_one[head] - lse)
        dprob = matmul(grad_head, v_ref[:, lanes], (1, 1))
        dscore = (prob * (dprob - delta) * SCALE).astype(BF16)
        merge(sums_q, head, matmul(dscore, k_ref[:, lanes], (1, 0)), True)
        merge(sums_k, head, matmul(dscore, q_ref[:, lanes], (0, 0)), True)
        merge(sums_v, head, matmul(prob.astype(BF16), grad_low, (0, 0)), True)

    arrived(cot_all, 2)
    for chunk in range(3):
        for head in range(EARLY[chunk], EARLY[chunk + 1]):
            one_back(head)
        arrived(att_all.at[chunk], 13 + chunk)
        part[chunk] = matmul(
            cot_all[...].reshape(4 * ROWS, HALF), att_all[chunk].reshape(4 * ROWS, 128), (0, 0)
        )
        if chunk < 2:
            for other in range(8):
                near = part[chunk, 24 * other : 24 * other + 24]
                far = part[chunk, 192 + 24 * other : 216 + 24 * other]
                z_send[chunk, other] = jnp.concatenate([near, far], axis=0).astype(BF16)
            for step in (4, 3, 5, 2, 6, 1, 7):
                other = (z + step) % 8
                device = plane + 4 * other + y
                push(z_send.at[chunk, other], z_recv.at[chunk, z], 16 + chunk, device)
            keep(z_send.at[chunk, z], z_recv.at[chunk, z], 16 + chunk)

    for other in range(4):
        for group in range(16):
            start = 24 * group + 6 * other
            last_rows[8 * group : 8 * group + 6] = part[2, start : start + 6]
            last_rows[8 * group + 6 : 8 * group + 8] = jnp.zeros((2, 128), F32)
        last_send[other] = last_rows[...].astype(BF16)

    @pl.loop(1, 4)
    def _(step):
        other = (y + step) % 4
        push(last_send.at[other], last_recv.at[y], 18, plane + 4 * z + other)

    keep(last_send.at[y], last_recv.at[y], 18)

    @pl.when(has_head)
    def _():
        arrived(stat_recv_three, 7)
        first, turned, value_rows = split_three()
        stats = stat_recv_three[...].reshape(256, 128)
        grad_rows = part_of(pltpu.roll(stats, 64, 1), 0)
        prob = jnp.exp(scores_three[...] - stats[:, 0:1])
        dprob = matmul(grad_rows, value_rows, (1, 1))
        dscore = (prob * (dprob - stats[:, 32:33]) * SCALE).astype(BF16)
        grad_qk = matmul(dscore, part_of(turned, 0), (1, 0))
        grad_qk = grad_qk + matmul(dscore, part_of(turned, 64), (0, 0))
        grad_v = matmul(prob.astype(BF16), grad_rows, (0, 0))
        grads = jnp.concatenate([grad_qk.reshape(32, 8, 128), grad_v.reshape(32, 8, 128)], axis=1)
        grad_send_three[...] = grads.astype(BF16)

        @pl.loop(0, 31)
        def _(step):
            other = (mine_three + outward(step, 32)) % 32
            push(grad_send_three.at[other], grad_recv_three.at[own_head], 8, plane + other)

        keep(grad_send_three.at[mine_three], grad_recv_three.at[own_head], 8)

    arrived(d_recv_two, 12)
    arrived(stat_recv_two, 6)
    row = iota((128, 256), 0)
    stats = stat_recv_two[...]
    grads = [None] * 3
    for member in range(2):

        def gathered(first):
            hit = (row == first) | (row == first + 8) | (row == first + 16)
            return matmul(stats, jnp.where(hit, 1.0, 0.0).astype(BF16), (1, 0))

        prob = jnp.exp(scores_two[member] - gathered(DIM * member))
        dprob = matmul(masked(d_recv_two[...], DIM * member, DIM), recv_two[2], (1, 1))
        dscore = (prob * (dprob - gathered(DIM * member + 24)) * SCALE).astype(BF16)
        news = (
            matmul(dscore, recv_two[1], (1, 0)),
            matmul(dscore, recv_two[0], (0, 0)),
            matmul(prob.astype(BF16), d_recv_two[...], (0, 0)),
        )
        for index, new in enumerate(news):
            old = grads[index]
            grads[index] = new if member == 0 else jnp.where(lanes_two < DIM, old, new)
    for index in range(3):
        grad_send_two[index] = grads[index].astype(BF16)

    @pl.loop(1, 8)
    def _(step):
        other = (mine_two + step) % 8
        push(grad_send_two.at[:, pl.ds(32 * other, 32)], grad_recv_two.at[mine_two], 9, block + other)

    keep(grad_send_two.at[:, pl.ds(32 * mine_two, 32)], grad_recv_two.at[mine_two], 9)

    arrived(last_recv, 18)
    rows = (last_recv[0].astype(F32) + last_recv[1].astype(F32)) + (
        last_recv[2].astype(F32) + last_recv[3].astype(F32)
    )
    w_send[...] = rows.reshape(16, 8, 128)

    @pl.loop(0, 15)
    def _(step):
        other = (8 * x_low + z + outward(step, 16)) % 16
        low, high = other // 8, other % 8
        device = (2 * x_high + low) * 32 + 4 * high + y
        push(w_send.at[other], w_recv.at[8 * x_low + z], 10, device)

    keep(w_send.at[8 * x_low + z], w_recv.at[8 * x_low + z], 10)
    for chunk in range(2):
        arrived(z_recv.at[chunk], 16 + chunk)
        rows = z_recv[chunk, 0].astype(F32)
        for other in range(1, 8):
            rows = rows + z_recv[chunk, other].astype(F32)
        block_rows[:, 128 * chunk : 128 * chunk + 128] = rows
    for low in range(2):
        for other in range(4):
            start = 24 * low + 6 * other
            y_send[low, other, 0:6] = block_rows[start : start + 6]
            y_send[low, other, 6:8] = jnp.zeros((2, 256), F32)

    @pl.loop(1, 8)
    def _(step):
        other = (4 * x_low + y + step) % 8
        low, high = other // 4, other % 4
        device = (2 * x_high + low) * 32 + 4 * z + high
        push(y_send.at[low, high], y_recv.at[x_low, y], 11, device)

    keep(y_send.at[x_low, y], y_recv.at[x_low, y], 11)

    attended = jnp.concatenate([att_halves[tile // 3, tile % 3] for tile in range(TILES)], axis=1)
    mixed_ref[...] = matmul(attended, weight_ref[...], (1, 1)).astype(BF16)
    outgoing[0].start()
    for head in range(EARLY[3], HEADS):
        one_back(head)
    for tile in range(TILES):
        totals[0, tile] = sums_q[tile]
        totals[1, tile] = sums_k[tile]
        totals[2, tile] = sums_v[tile]

    arrived(grad_recv_three, 8)
    received = grad_recv_three[...].astype(F32)
    for index, (place, rows) in enumerate(((0, slice(0, 8)), (64, slice(0, 8)), (0, slice(8, 16)))):
        tiles = put_windows([received[head, rows] for head in range(HEADS)], DIM, place)
        spread(totals.at[index], 1, tiles, True)
    arrived(grad_recv_two, 9)
    for index, out_ref in enumerate((dq_ref, dk_ref, dv_ref)):
        windows = [grad_recv_two[other, index].astype(F32) for other in range(8)]
        spread(totals.at[index], 0, put_windows(windows, 96, 0), True)
        for tile in range(TILES):
            out_ref[:, 128 * tile : 128 * tile + 128] = totals[index, tile].astype(BF16)
        outgoing[1 + index].start()

    arrived(y_recv, 11)
    for low in range(2):
        rows = (y_recv[low, 0] + y_recv[low, 1]) + (y_recv[low, 2] + y_recv[low, 3])
        dw_ref[:, HALF * low : HALF * low + 256] = rows[0:6] * (16384**-0.5)
    arrived(w_recv, 10)
    for low in range(2):
        rows = w_recv[8 * low]
        for other in range(1, 8):
            rows = rows + w_recv[8 * low + other]
        dw_ref[:, HALF * low + 256 : HALF * low + HALF] = rows[0:6] * (16384**-0.5)
    outgoing[4].start()

    left(send_two.at[0:7], 0)
    left(cot_all.at[0:3], 2)
    left(out_send_two.at[0:224], 4)
    for chunk in range(3):
        left(att_all.at[chunk, 0:3], 13 + chunk)
    left(stat_send_two.at[0:7], 6)
    left(grad_recv_two.at[0:7], 9)
    left(d_send_two.at[0:7], 12)
    left(z_send.at[0, 0:7], 16)
    left(z_send.at[1, 0:7], 17)
    left(last_send.at[0:3], 18)
    left(w_send.at[0:15], 10)
    left(y_send.at[0:1], 11)
    left(y_send.at[0, 0:3], 11)

    @pl.when(has_head)
    def _():
        left(send_three.at[0:15], 1)
        left(stat_send_three.at[0:15], 7)
        left(out_send_three.at[0:31], 3)
        left(grad_send_three.at[0:31], 8)

    @pl.when(jnp.logical_not(has_head))
    def _():
        left(send_three, 1)
        left(stat_send_three, 7)

    for copy in outgoing:
        copy.wait()


def finish(*refs):
    sources, results, holders, sems = refs[:5], refs[5:10], refs[10:15], refs[15]
    inward, outward = [], []
    for index in range(5):
        inward.append(pltpu.make_async_copy(sources[index], holders[index], sems.at[0, index]))
        outward.append(pltpu.make_async_copy(holders[index], results[index], sems.at[1, index]))
        inward[index].start()
    for index in range(5):
        inward[index].wait()
        outward[index].start()
    for index in range(5):
        outward[index].wait()


def local(queries, keys, values, cotangent, out_weight, slide_lengths, head_dilation_shifts):
    far = pl.BlockSpec(memory_space=pltpu.HBM)
    wide = jax.ShapeDtypeStruct((ROWS, WIDTH), BF16)
    scratch = [
        ((4, TILES, ROWS, 128), F32),
        ((8, 3, 32, 128), BF16),
        ((3, 256, 128), BF16),
        ((8, 32, 128), BF16),
        ((256, 128), BF16),
        ((16, 16, 128), BF16),
        ((32, 16, 128), BF16),
        ((256, 128), BF16),
        ((8, 32, 128), BF16),
        ((32, 8, 128), F32),
        ((16, 8, 128), F32),
        ((8, 32, 128), BF16),
        ((256, 128), BF16),
        ((16, 8, 128), F32),
        ((32, 8, 128), F32),
        ((3, 256, 128), BF16),
        ((8, 3, 32, 128), BF16),
        ((32, 16, 128), BF16),
        ((16, 16, 128), BF16),
        ((2, ROWS, HALF), BF16),
        ((2, 3, ROWS, 128), BF16),
        ((4, ROWS, HALF), BF16),
        ((3, 4, ROWS, 128), BF16),
        ((3, HALF, 128), F32),
        ((48, 256), F32),
        ((2, 8, 48, 128), BF16),
        ((2, 8, 48, 128), BF16),
        ((HALF, HALF), BF16),
        ((128, 128), BF16),
        ((128, 128), F32),
        ((4, 128, 128), BF16),
        ((4, 128, 128), BF16),
        ((16, 8, 128), F32),
        ((16, 8, 128), F32),
        ((2, 4, 8, 256), F32),
        ((2, 4, 8, 256), F32),
        ((HEADS, ROWS, ROWS), F32),
        ((2, 256, 256), F32),
        ((256, 256), F32),
        ((3, TILES, ROWS, 128), F32),
        ((3, TILES, ROWS, 128), F32),
        ((TILES, ROWS, 128), F32),
        ((TILES, ROWS, 128), F32),
        ((3, TILES, ROWS, 128), F32),
    ]
    out_shape = (wide, wide, wide, wide, jax.ShapeDtypeStruct((WIDTH // 128, WIDTH), F32))
    results = pl.pallas_call(
        kernel,
        out_shape=out_shape,
        in_specs=[far] * 7,
        out_specs=(far,) * 5,
        scratch_shapes=[pltpu.VMEM((ROWS, WIDTH), BF16)] * 4
        + [pltpu.VMEM((WIDTH // 128, WIDTH), F32)]
        + [pltpu.VMEM((ROWS, WIDTH), BF16)] * 4
        + [pltpu.VMEM((WIDTH, WIDTH), BF16), pltpu.SMEM((8,), jnp.int32), pltpu.SMEM((2, HEADS), jnp.int32)]
        + [pltpu.VMEM(shape, dtype) for shape, dtype in scratch]
        + [pltpu.SemaphoreType.DMA((19,)), pltpu.SemaphoreType.DMA((19,)), pltpu.SemaphoreType.DMA((7,)), pltpu.SemaphoreType.DMA((5,))],
        compiler_params=pltpu.CompilerParams(
            collective_id=0, has_side_effects=True, vmem_limit_bytes=VMEM
        ),
        name="dilated_attention",
    )(queries, keys, values, cotangent, out_weight, slide_lengths, head_dilation_shifts)
    return pl.pallas_call(
        finish,
        out_shape=out_shape,
        in_specs=[far] * 5,
        out_specs=(far,) * 5,
        scratch_shapes=[pltpu.VMEM(shape.shape, shape.dtype) for shape in out_shape]
        + [pltpu.SemaphoreType.DMA((2, 5))],
        compiler_params=pltpu.CompilerParams(vmem_limit_bytes=VMEM),
        name="results_to_hbm",
    )(*results)


def solution(mesh):
    rows = P(("dp", "seq"), None)
    return jax.shard_map(
        local,
        mesh=mesh,
        in_specs=(rows, rows, rows, rows, P(), P("dp"), P()),
        out_specs=(rows,) * 5,
        check_vma=False,
    )
```
